128 devices in a mesh: tm: 4 (over x_hi, core), height: 32 (over y, x_lo, z).
Axes of the slice: x: 4 (x_hi: 2, x_lo: 2; x = x_hi * 2 + x_lo), y: 4, z: 4, core: 2. Of those that a mesh axis runs over, the one named last changes fastest.
Arguments:
- tokens: bfloat16 [32, 448, 14, 256], P('tm', 'height'), may hold values from -6 to 6
- region_ids: int32 [32, 448, 14], P('tm', 'height'), may hold values from 0 to 26, as said below
- first_gain: float32 [256], replicated, may hold values from 0.5 to 1.5
- first_bias: float32 [256], replicated, may hold values from -1.5 to 1.5
- input_weight: bfloat16 [256, 768], replicated, may hold values from -0.375 to 0.375
- input_bias: float32 [768], replicated, may hold values from -1.5 to 1.5
- output_weight: bfloat16 [256, 256], replicated, may hold values from -0.375 to 0.375
- output_bias: float32 [256], replicated, may hold values from -1.5 to 1.5
- second_gain: float32 [256], replicated, may hold values from 0.5 to 1.5
- second_bias: float32 [256], replicated, may hold values from -1.5 to 1.5
- expand_weight: bfloat16 [256, 1024], replicated, may hold values from -0.375 to 0.375
- expand_bias: float32 [1024], replicated, may hold values from -1.5 to 1.5
- reduce_weight: bfloat16 [1024, 256], replicated, may hold values from -0.1875 to 0.1875
- reduce_bias: float32 [256], replicated, may hold values from -1.5 to 1.5
- merge_gain: float32 [1024], replicated, may hold values from 0.5 to 1.5
- merge_bias: float32 [1024], replicated, may hold values from -1.5 to 1.5
- merge_weight: bfloat16 [1024, 512], replicated, may hold values from -0.1875 to 0.1875
- cotangent: bfloat16 [32, 224, 7, 512], P(None, 'height', None, 'tm'), may hold values from -6 to 6
Outputs:
- merged: bfloat16 [32, 224, 7, 512], P(None, 'height', None, 'tm')
- grad_tokens: bfloat16 [32, 448, 14, 256], P('tm', 'height')
- grad_first_gain: float32 [256], replicated
- grad_first_bias: float32 [256], replicated
- grad_input_weight: float32 [256, 768], replicated
- grad_input_bias: float32 [768], replicated
- grad_output_weight: float32 [256, 256], replicated
- grad_output_bias: float32 [256], replicated
- grad_second_gain: float32 [256], replicated
- grad_second_bias: float32 [256], replicated
- grad_expand_weight: float32 [256, 1024], replicated
- grad_expand_bias: float32 [1024], replicated
- grad_reduce_weight: float32 [1024, 256], replicated
- grad_reduce_bias: float32 [256], replicated
- grad_merge_gain: float32 [1024], replicated
- grad_merge_bias: float32 [1024], replicated
- grad_merge_weight: float32 [1024, 512], replicated
The draws below stay inside these ranges and needn't reach their ends.
Inputs may be any that keep to these rules, and one draw needn't show every extreme that they name: `region_ids`: swin shift-region labels of the shifted grid: 9 a + 3 b + c, where a, b, c in 0 to 2 tell in which slab a cell's frame, row and column lies ([0, n - w), [n - w, n - w / 2), [n - w / 2, n) for a dimension of n cells and windows of w cells); about one cell in eight holds an arbitrary label instead.
All inputs are finite; a program needn't handle non-finite values.
Results may differ from the reference program's by a relative error of at most 0.024.
Values may be sent and summed in bfloat16 or wider, within the bound.
No kernel may reach another device: no remote copies, remote signals or barrier semaphores. Data moves between devices by JAX's collectives and lax.ppermute only.
A program may use at most 128 MiB of HBM per device.

```python
import math
import jax
import jax.numpy as jnp
from jax import lax

DIM = 256
HEADS = 8
HIDDEN_SIZE = 1024
WIN_T = 8
WIN_H = 7
WIN_W = 7
WIDTH = 14
FRAMES = 32
HEIGHT = 448
MROWS = 224
MCOLS = 7
N_TM = 4
N_HEIGHT = 32


def slab_index(position, length, window):
    return jnp.where(position < length - window, 0, jnp.where(position < length - window // 2, 1, 2))


def draw_region_ids(key, part):
    key = jax.random.fold_in(key, 11)
    shape = (FRAMES, HEIGHT, WIDTH)
    frame_pos = lax.broadcasted_iota(jnp.int32, shape, 0)
    row_pos = lax.broadcasted_iota(jnp.int32, shape, 1)
    col_pos = lax.broadcasted_iota(jnp.int32, shape, 2)
    base = 9 * slab_index(frame_pos, FRAMES, WIN_T) + 3 * slab_index(row_pos, HEIGHT, WIN_H) + slab_index(col_pos, WIDTH, WIN_W)
    flip_key = jax.random.fold_in(key, 1)
    value_key = jax.random.fold_in(key, 2)
    flipped = jax.random.randint(flip_key, shape, 0, 8) == 0
    first_cell = jnp.logical_and(jnp.logical_and(frame_pos == 0, row_pos == 0), col_pos == 0)
    last_cell = jnp.logical_and(jnp.logical_and(frame_pos == FRAMES - 1, row_pos == HEIGHT - 1), col_pos == WIDTH - 1)
    kept = jnp.logical_or(first_cell, last_cell)
    noise = jax.random.randint(value_key, shape, 0, 27)
    return jnp.where(jnp.logical_and(flipped, jnp.logical_not(kept)), noise, base).astype(jnp.int32)


def shard_levels(stream_key, dims, shards, smallest, high):
    def one(dim, parts):
        steps = jax.random.uniform(jax.random.fold_in(jax.random.fold_in(stream_key, 6), dim), (parts,), jnp.float32, smallest / len(shards), high / len(shards))
        return jnp.repeat(jnp.exp(steps), dims[dim] // parts).reshape((-1,) + (1,) * (len(dims) - dim - 1))

    loudness = one(*shards[0])
    for cut in shards[1:]:
        loudness = loudness * one(*cut)
    return loudness


def gaussian(key, dims, spread, reach, pieces=(), kind=jnp.bfloat16):
    result = jax.random.normal(key, dims, jnp.float32) * spread
    if len(pieces) > 0:
        result = shard_levels(key, dims, pieces, -0.22, 0.18) * result
    return jnp.clip(result, min=-reach, max=reach).astype(kind)


def setup_inputs(seed: int = 0) -> dict:
    seeds = jax.random.split(jax.random.key(seed), 19)
    tokens = gaussian(seeds[0], (FRAMES, HEIGHT, WIDTH, DIM), 1.0, 6.0, ((0, 4), (1, 32)))
    region_ids = draw_region_ids(jax.random.fold_in(seeds[18], 71), 0)
    first_gain = jnp.clip(1.0 + 0.1 * jax.random.normal(seeds[2], (DIM,), jnp.float32), 0.5, 1.5)
    first_bias = gaussian(seeds[3], (DIM,), 0.3, 1.5, (), jnp.float32)
    input_weight = gaussian(seeds[4], (DIM, 3 * DIM), DIM ** -0.5, 0.375)
    input_bias = gaussian(seeds[5], (3 * DIM,), 0.3, 1.5, (), jnp.float32)
    output_weight = gaussian(seeds[6], (DIM, DIM), DIM ** -0.5, 0.375)
    output_bias = gaussian(seeds[7], (DIM,), 0.3, 1.5, (), jnp.float32)
    second_gain = jnp.clip(1.0 + 0.1 * jax.random.normal(seeds[8], (DIM,), jnp.float32), 0.5, 1.5)
    second_bias = gaussian(seeds[9], (DIM,), 0.3, 1.5, (), jnp.float32)
    expand_weight = gaussian(seeds[10], (DIM, HIDDEN_SIZE), DIM ** -0.5, 0.375)
    expand_bias = gaussian(seeds[11], (HIDDEN_SIZE,), 0.3, 1.5, (), jnp.float32)
    reduce_weight = gaussian(seeds[12], (HIDDEN_SIZE, DIM), HIDDEN_SIZE ** -0.5, 0.1875)
    reduce_bias = gaussian(seeds[13], (DIM,), 0.3, 1.5, (), jnp.float32)
    merge_gain = jnp.clip(1.0 + 0.1 * jax.random.normal(seeds[14], (4 * DIM,), jnp.float32), 0.5, 1.5)
    merge_bias = gaussian(seeds[15], (4 * DIM,), 0.3, 1.5, (), jnp.float32)
    merge_weight = gaussian(seeds[16], (4 * DIM, 2 * DIM), (4 * DIM) ** -0.5, 0.1875)
    cotangent = gaussian(seeds[17], (FRAMES, MROWS, MCOLS, 2 * DIM), 1.0, 6.0, ((1, 32), (3, 4)))
    return {"tokens": tokens, "region_ids": region_ids, "first_gain": first_gain, "first_bias": first_bias, "input_weight": input_weight, "input_bias": input_bias, "output_weight": output_weight, "output_bias": output_bias, "second_gain": second_gain, "second_bias": second_bias, "expand_weight": expand_weight, "expand_bias": expand_bias, "reduce_weight": reduce_weight, "reduce_bias": reduce_bias, "merge_gain": merge_gain, "merge_bias": merge_bias, "merge_weight": merge_weight, "cotangent": cotangent}


NORM_EPS = 1e-05

def layer_norm(inputs, norm_gain, norm_bias):
    widened = inputs.astype(jnp.float32)
    average = lax.optimization_barrier(jnp.mean(widened, -1, keepdims=True))
    centred = widened - average
    variance = lax.optimization_barrier(jnp.mean(centred * centred, -1, keepdims=True))
    return (centred * lax.rsqrt(variance + NORM_EPS) * norm_gain + norm_bias).astype(jnp.bfloat16)

def window_core(queries, keys_in, values_in, labels):
    factor = queries.shape[-1] ** (-0.5)
    scores = jnp.einsum('gqhd,gkhd->ghqk', queries.astype(jnp.float32), keys_in.astype(jnp.float32)) * factor
    allowed = (labels[:, :, None] == labels[:, None, :])[:, None]
    weights = jnp.where(allowed, jnp.exp(scores), 0.0)
    probs = (weights / lax.optimization_barrier(jnp.sum(weights, -1, keepdims=True))).astype(jnp.bfloat16)
    return jnp.einsum('ghqk,gkhd->gqhd', probs.astype(jnp.float32), values_in.astype(jnp.float32)).astype(jnp.bfloat16)

def attend_block(shifted, region_block, input_weight, input_bias, output_weight, output_bias):
    frames, row_total, col_total, channels = shifted.shape
    row_wins = row_total // WIN_H
    col_wins = col_total // WIN_W
    count = row_wins * col_wins
    window_size = frames * WIN_H * WIN_W
    head_width = channels // HEADS
    windows = shifted.reshape(frames, row_wins, WIN_H, col_wins, WIN_W, channels)
    windows = windows.transpose(1, 3, 0, 2, 4, 5).reshape(count * window_size, channels)
    labels = region_block.reshape(frames, row_wins, WIN_H, col_wins, WIN_W)
    labels = labels.transpose(1, 3, 0, 2, 4).reshape(count // 2, 2, window_size)
    packed = (jnp.dot(windows, input_weight, preferred_element_type=jnp.float32) + input_bias).astype(jnp.bfloat16)
    packed = packed.reshape(count // 2, 2, window_size, 3, HEADS, head_width)
    checked = jax.checkpoint(window_core)
    context = lax.map(lambda grouped: checked(grouped[0], grouped[1], grouped[2], grouped[3]), (packed[:, :, :, 0], packed[:, :, :, 1], packed[:, :, :, 2], labels))
    context = context.reshape(count * window_size, channels)
    output = (jnp.dot(context, output_weight, preferred_element_type=jnp.float32) + output_bias).astype(jnp.bfloat16)
    output = output.reshape(row_wins, col_wins, frames, WIN_H, WIN_W, channels)
    return output.transpose(2, 0, 3, 1, 4, 5).reshape(frames, row_total, col_total, channels)

def post_block(block_tokens, restored, second_gain, second_bias, expand_weight, expand_bias, reduce_weight, reduce_bias, merge_gain, merge_bias, merge_weight):
    frames, row_total, col_total, channels = block_tokens.shape
    residual = (block_tokens.astype(jnp.float32) + restored.astype(jnp.float32)).astype(jnp.bfloat16)
    residual = residual.reshape(-1, channels)
    second_normed = layer_norm(residual, second_gain, second_bias)
    hidden = jax.nn.gelu(jnp.dot(second_normed, expand_weight, preferred_element_type=jnp.float32) + expand_bias, approximate=False).astype(jnp.bfloat16)
    block_out = (residual.astype(jnp.float32) + jnp.dot(hidden, reduce_weight, preferred_element_type=jnp.float32) + reduce_bias).astype(jnp.bfloat16)
    quadrants = block_out.reshape(frames, row_total // 2, 2, col_total // 2, 2, channels)
    gathered = jnp.concatenate([quadrants[:, :, 0, :, 0], quadrants[:, :, 1, :, 0], quadrants[:, :, 0, :, 1], quadrants[:, :, 1, :, 1]], -1)
    merge_normed = layer_norm(gathered, merge_gain, merge_bias)
    merged = jnp.dot(merge_normed.reshape(-1, 4 * channels), merge_weight, preferred_element_type=jnp.float32).astype(jnp.bfloat16)
    return merged.reshape(frames, row_total // 2, col_total // 2, 2 * channels)

def to_blocks(whole):
    first_len = whole.shape[0] // N_TM
    second_len = whole.shape[1] // N_HEIGHT
    remaining = whole.shape[2:]
    split_up = whole.reshape((N_TM, first_len, N_HEIGHT, second_len) + remaining)
    split_up = jnp.swapaxes(split_up, 1, 2)
    return split_up.reshape((N_TM * N_HEIGHT, first_len, second_len) + remaining)

def from_blocks(blocks):
    first_len = blocks.shape[1]
    second_len = blocks.shape[2]
    remaining = blocks.shape[3:]
    split_up = blocks.reshape((N_TM, N_HEIGHT, first_len, second_len) + remaining)
    split_up = jnp.swapaxes(split_up, 1, 2)
    return split_up.reshape((N_TM * first_len, N_HEIGHT * second_len) + remaining)

def reference(tokens, region_ids, first_gain, first_bias, input_weight, input_bias, output_weight, output_bias, second_gain, second_bias, expand_weight, expand_bias, reduce_weight, reduce_bias, merge_gain, merge_bias, merge_weight, cotangent):
    block_count = N_TM * N_HEIGHT

    def copies(param):
        return jnp.broadcast_to(param, (block_count,) + param.shape)
    norm_params = (copies(first_gain), copies(first_bias))
    attn_params = (copies(input_weight), copies(input_bias), copies(output_weight), copies(output_bias))
    post_params = (copies(second_gain), copies(second_bias), copies(expand_weight), copies(expand_bias), copies(reduce_weight), copies(reduce_bias), copies(merge_gain), copies(merge_bias), copies(merge_weight))
    label_blocks = to_blocks(region_ids)
    attend_checked = jax.checkpoint(attend_block)
    post_checked = jax.checkpoint(post_block)

    def forward(token_in, norm_set, attn_set, post_set):
        token_blocks = to_blocks(token_in)
        normed = from_blocks(lax.map(lambda item: layer_norm(item[0], item[1], item[2]), (token_blocks,) + norm_set))
        shifted = jnp.roll(normed, (-(WIN_T // 2), -(WIN_H // 2), -(WIN_W // 2)), (0, 1, 2))
        attended = from_blocks(lax.map(lambda item: attend_checked(item[0], item[1], item[2], item[3], item[4], item[5]), (to_blocks(shifted), label_blocks) + attn_set))
        restored = jnp.roll(attended, (WIN_T // 2, WIN_H // 2, WIN_W // 2), (0, 1, 2))
        return lax.map(lambda item: post_checked(item[0], item[1], item[2], item[3], item[4], item[5], item[6], item[7], item[8], item[9], item[10]), (token_blocks, to_blocks(restored)) + post_set)
    merged_blocks, backward = jax.vjp(forward, tokens, norm_params, attn_params, post_params)
    merged = from_blocks(merged_blocks)
    grad_tokens, norm_grads, attn_grads, post_grads = backward(to_blocks(cotangent))
    factor = 1.0 / math.sqrt(FRAMES * MROWS * MCOLS)
    sums = [lax.optimization_barrier(jnp.sum(grad_part.astype(jnp.float32), 0)) * factor for grad_part in tuple(norm_grads) + tuple(attn_grads) + tuple(post_grads)]
    return (merged, grad_tokens, sums[0], sums[1], sums[2], sums[3], sums[4], sums[5], sums[6], sums[7], sums[8], sums[9], sums[10], sums[11], sums[12], sums[13], sums[14])
```

```python
import functools
import math

import jax
import jax.numpy as jnp
from jax import lax
from jax.experimental import pallas as pl
from jax.experimental.pallas import tpu as pltpu
from jax.sharding import PartitionSpec as P

F32 = jnp.float32
BF16 = jnp.bfloat16
NORM_EPS = 1e-05
DIM = 256
CELLS = 392
TILES = 49
FAR = 2.0**100
SCORE_SCALE = math.log2(math.e) / math.sqrt(32.0)
MIB = 1 << 20


def dot(a, b):
    return lax.dot_general(a, b, (((1,), (0,)), ((), ())), preferred_element_type=F32)


def dot_nt(a, b):
    return lax.dot_general(a, b, (((1,), (1,)), ((), ())), preferred_element_type=F32)


def dot_tn(a, b):
    return lax.dot_general(a, b, (((0,), (0,)), ((), ())), preferred_element_type=F32)


def row(ref):
    return ref[...].reshape(1, -1)


def norm_stats(x):
    average = jnp.mean(x, -1, keepdims=True)
    centred = x - average
    rstd = lax.rsqrt(jnp.mean(centred * centred, -1, keepdims=True) + NORM_EPS)
    return centred * rstd, rstd


def norm_back(dxhat, xhat, rstd):
    first = jnp.mean(dxhat, -1, keepdims=True)
    second = jnp.mean(dxhat * xhat, -1, keepdims=True)
    return (dxhat - first - xhat * second) * rstd


def lanes(rows):
    return lax.broadcasted_iota(jnp.int32, (rows, 128), 1)


def head_mask(index):
    return (lanes(1) // 32 == index).astype(BF16)


def three_parts(value, lane, start):
    high = value.astype(BF16).astype(F32)
    middle = (value - high).astype(BF16).astype(F32)
    low = value - high - middle
    return jnp.where(lane < start + 8, high, jnp.where(lane < start + 16, middle, low))


def attend_kernel(
    tok_ref, lab_ref, gain_ref, bias_ref, wi_ref, bi_ref, wo_ref, bo_ref,
    res_ref, x_ref, qkv_ref, ctx_ref, eq_ref, field,
):
    for f in range(8):
        for r in range(7):
            start = (f * 7 + r) * 16
            cells = tok_ref[f, r].astype(F32)
            for half in range(2):
                field[half, start : start + 14, :] = cells[:, 128 * half : 128 * half + 128]

    def window(win, carry):
        parts = []
        for wi in range(7):
            for wj in range(7):
                column = lax.rem(win * 7 + wj + 3, 14)
                parts.append(
                    jnp.concatenate(
                        [field[s, pl.ds(wi * 16 + column, 8, stride=112), :] for s in range(2)],
                        1,
                    )
                )
        x = jnp.concatenate(parts, 0)
        x_ref[win] = x.astype(BF16)
        xhat, _ = norm_stats(x)
        normed = (xhat * row(gain_ref) + row(bias_ref)).astype(BF16)
        packed = dot(normed, wi_ref[...]) + row(bi_ref)
        q = (packed[:, 0:256] * SCORE_SCALE).astype(BF16)
        k = packed[:, 256:512].astype(BF16)
        v = packed[:, 512:768]
        vb = v.astype(BF16)
        vs = (v * (2.0**-12)).astype(BF16)
        qkv_ref[win, :, 0:256] = q
        qkv_ref[win, :, 256:512] = k
        qkv_ref[win, :, 512:768] = vb
        label = lab_ref[win]
        lane = lanes(CELLS)
        same = lane == label
        eq32 = jnp.where(same | (lane == 27), 1.0, 0.0)
        eq = eq32.astype(BF16)
        ek = jnp.where(
            lane < 27, jnp.where(same, 0.0, -FAR), jnp.where(lane == 27, -1.0, 0.0)
        ).astype(BF16)
        ones = jnp.ones((CELLS, 128), BF16)
        sums = jnp.ones((CELLS, 128), F32)
        halves = []
        for t in range(2):
            qt = q[:, 128 * t : 128 * t + 128]
            kaug = jnp.concatenate([k[:, 128 * t : 128 * t + 128], ek], 1)
            vaug = jnp.concatenate([vs[:, 128 * t : 128 * t + 128], ones], 1)
            half = jnp.zeros((CELLS, 128), F32)
            for hh in range(4):
                h = 4 * t + hh
                qaug = jnp.concatenate([qt * head_mask(hh), eq], 1)
                p = jnp.exp2(dot_nt(qaug, kaug)).astype(BF16)
                pv = dot(p, vaug)
                total = pv[:, 128:256]
                half = jnp.where(lane // 32 == hh, pv[:, 0:128] * (4096.0 / total), half)
                sums = jnp.where((lane >= 32) & (lane < 56) & (lane % 8 == h), total, sums)
            halves.append(half)
        ctx = jnp.concatenate(halves, 1).astype(BF16)
        ctx_ref[win] = ctx
        minus = three_parts(-jnp.log2(sums), lane, 32)
        eq_ref[win] = jnp.where((lane >= 32) & (lane < 56), minus, eq32).astype(BF16)
        attended = (dot(ctx, wo_ref[...]) + row(bo_ref)).astype(BF16)
        res_ref[win] = (x + attended.astype(F32)).astype(BF16)
        return carry

    lax.fori_loop(0, 2, window, 0)


def whole(shape):
    return pl.BlockSpec(shape, lambda i, n=len(shape): (0,) * n)


def attend(row_win, field, labels, gain, bias, wi, bi, wo, bo):
    outs = [(2, CELLS, 256), (2, CELLS, 256), (2, CELLS, 768), (2, CELLS, 256), (2, CELLS, 128)]
    return pl.pallas_call(
        attend_kernel,
        grid=(1,),
        in_specs=[
            pl.BlockSpec((8, 7, 14, 256), lambda i: (0, row_win, 0, 0)),
            pl.BlockSpec((2, CELLS, 1), lambda i: (row_win, 0, 0)),
            whole((256,)),
            whole((256,)),
            whole((256, 768)),
            whole((768,)),
            whole((256, 256)),
            whole((256,)),
        ],
        out_specs=[whole(s) for s in outs],
        out_shape=[jax.ShapeDtypeStruct(s, BF16) for s in outs],
        scratch_shapes=[pltpu.VMEM((2, 896, 128), F32)],
        compiler_params=pltpu.CompilerParams(vmem_limit_bytes=48 * MIB),
        cost_estimate=pl.CostEstimate(flops=8 * 10**9, bytes_accessed=8 * 10**6, transcendentals=2500000),
    )(field, labels, gain, bias, wi, bi, wo, bo)


def attend_back_kernel(
    d_ref, x_ref, qkv_ref, ctx_ref, eq_ref, lab_ref, gain_ref, bias_ref, wi_ref, wo_ref,
    out_ref, dwi_ref, dwo_ref, vec_ref, field, dwi, dwo, vec,
):
    dwi[...] = jnp.zeros_like(dwi)
    dwo[...] = jnp.zeros_like(dwo)
    vec[...] = jnp.zeros_like(vec)

    def window(win, carry):
        d = d_ref[win]
        d32 = d.astype(F32)
        ctx = ctx_ref[win]
        dwo[...] += dot_tn(ctx, d)
        vec[3:4, 0:256] += jnp.sum(d32, 0, keepdims=True)
        dctx = dot_nt(d, wo_ref[...]).astype(BF16)
        product = dctx.astype(F32) * ctx.astype(F32)
        high = product.astype(BF16)
        low = (product - high.astype(F32)).astype(BF16)
        picks_r = lax.broadcasted_iota(jnp.int32, (256, 128), 0) // 32
        picks_c = lax.broadcasted_iota(jnp.int32, (256, 128), 1)
        picks = ((picks_c < 24) & (picks_c % 8 == picks_r)).astype(BF16)
        lane = lanes(CELLS)
        delta = three_parts(-(dot(high, picks) + dot(low, picks)), lane, 0)
        dd = jnp.where(lane < 24, delta, 0.0).astype(BF16)
        eq = eq_ref[win]
        same = lane == lab_ref[win]
        ek = jnp.where(lane < 27, jnp.where(same, 0.0, -FAR), jnp.where(lane == 27, -1.0, 0.0))
        lane1 = lanes(1)
        dqs, dks, dvs = [], [], []
        for t in range(2):
            cols = slice(128 * t, 128 * t + 128)
            qt = qkv_ref[win, :, 128 * t : 128 * t + 128]
            kt = qkv_ref[win, :, 256 + 128 * t : 256 + 128 * t + 128]
            vt = qkv_ref[win, :, 512 + 128 * t : 512 + 128 * t + 128]
            dot_t = dctx[:, cols]
            qaug = jnp.concatenate([qt, eq], 1)
            daug = jnp.concatenate([dot_t, dd], 1)
            ktt = jnp.transpose(kt.astype(F32)).astype(BF16)
            dk = jnp.zeros((CELLS, 128), F32)
            dv = jnp.zeros((CELLS, 128), F32)
            dqt = []
            for hh in range(4):
                h = 4 * t + hh
                mask = head_mask(hh)
                picked = (lane1 >= 32) & (lane1 < 56) & (lane1 % 8 == h)
                kaug = jnp.concatenate([kt * mask, jnp.where(picked, 1.0, ek).astype(BF16)], 1)
                tail = jnp.where((lane < 24) & (lane % 8 == h), 1.0, 0.0).astype(BF16)
                vaug = jnp.concatenate([vt * mask, tail], 1)
                p = jnp.exp2(dot_nt(kaug, qaug))
                ds = (p * dot_nt(vaug, daug)).astype(BF16)
                dv = dv + dot(p.astype(BF16), dot_t * mask)
                dk = dk + dot(ds, qt * mask)
                dqt.append(dot(ktt[32 * hh : 32 * hh + 32, :], ds))
            dqs.append(jnp.transpose(jnp.concatenate(dqt, 0)))
            dks.append(dk)
            dvs.append(dv)
        dpacked32 = jnp.concatenate(
            [d_q * (1.0 / math.sqrt(32.0)) for d_q in dqs]
            + [d_k * math.log(2.0) for d_k in dks]
            + dvs,
            1,
        )
        dpacked = dpacked32.astype(BF16)
        vec[2:3, :] += jnp.sum(dpacked32, 0, keepdims=True)
        x = x_ref[win].astype(F32)
        xhat, rstd = norm_stats(x)
        gain = row(gain_ref)
        normed = (xhat * gain + row(bias_ref)).astype(BF16)
        dwi[...] += dot_tn(normed, dpacked)
        dnormed = dot_nt(dpacked, wi_ref[...]).astype(BF16).astype(F32)
        vec[0:1, 0:256] += jnp.sum(dnormed * xhat, 0, keepdims=True)
        vec[1:2, 0:256] += jnp.sum(dnormed, 0, keepdims=True)
        dx = norm_back(dnormed * gain, xhat, rstd).astype(BF16).astype(F32) + d32
        for wi in range(7):
            for wj in range(7):
                column = lax.rem(win * 7 + wj + 3, 14)
                at = (wi * 7 + wj) * 8
                for s in range(2):
                    field[s, pl.ds(wi * 16 + column, 8, stride=112), :] = dx[at : at + 8, 128 * s : 128 * s + 128]
        return carry

    lax.fori_loop(0, 2, window, 0)
    for f in range(8):
        for r in range(7):
            start = (f * 7 + r) * 16
            halves = [field[s, start : start + 14, :] for s in range(2)]
            out_ref[f, r] = jnp.concatenate(halves, 1).astype(BF16)
    for s in range(6):
        dwi_ref[s] = dwi[:, 128 * s : 128 * s + 128].astype(F32)
    for s in range(2):
        dwo_ref[s] = dwo[:, 128 * s : 128 * s + 128].astype(F32)
    vec_ref[...] = vec[...]


def attend_back(row_win, d, x, qkv, ctx, eq, labels, gain, bias, wi, wo):
    outs = [
        ((8, 7, 14, 256), BF16),
        ((6, 256, 128), F32),
        ((2, 256, 128), F32),
        ((8, 768), F32),
    ]
    return pl.pallas_call(
        attend_back_kernel,
        grid=(1,),
        in_specs=[
            whole((2, CELLS, 256)),
            whole((2, CELLS, 256)),
            whole((2, CELLS, 768)),
            whole((2, CELLS, 256)),
            whole((2, CELLS, 128)),
            pl.BlockSpec((2, CELLS, 1), lambda i: (row_win, 0, 0)),
            whole((256,)),
            whole((256,)),
            whole((256, 768)),
            whole((256, 256)),
        ],
        out_specs=[whole(s) for s, _ in outs],
        out_shape=[jax.ShapeDtypeStruct(s, t) for s, t in outs],
        scratch_shapes=[
            pltpu.VMEM((2, 896, 128), F32),
            pltpu.VMEM((256, 768), F32),
            pltpu.VMEM((256, 256), F32),
            pltpu.VMEM((8, 768), F32),
        ],
        compiler_params=pltpu.CompilerParams(vmem_limit_bytes=48 * MIB),
        cost_estimate=pl.CostEstimate(flops=20 * 10**9, bytes_accessed=8 * 10**6, transcendentals=2500000),
    )(d, x, qkv, ctx, eq, labels, gain, bias, wi, wo)


def gelu_pair(v):
    half_square = jnp.exp2(v * v * (-0.5 * math.log2(math.e)))
    t = 1.0 / (1.0 + jnp.abs(v) * (0.3275911 * math.sqrt(0.5)))
    poly = t * (0.5 * 0.254829592 + t * (0.5 * -0.284496736 + t * (0.5 * 1.421413741 + t * (0.5 * -1.453152027 + t * (0.5 * 1.061405429)))))
    tail = poly * half_square
    phi = jnp.where(v >= 0.0, 1.0 - tail, tail)
    return v * phi, phi + v * half_square * (1.0 / math.sqrt(2.0 * math.pi))


QUADRANTS = ((0, 0), (1, 0), (0, 1), (1, 1))


def tile_start(r, c):
    s = (c - 3) % 14
    return ((s // 7) * 14 + r) * 56 + (s % 7) * 8


def post_kernel(
    above_ref, res0_ref, res1_ref, cot_ref, sg_ref, sb_ref, we_ref, be_ref, wr_ref, br_ref, mg_ref, mb_ref, wm_ref,
    merged_ref, dabove_ref, d0_ref, d1_ref, dwe_ref, dwr_ref, dwm_ref, vec_ref,
    field, sn_all, hid_all, dbo_all, dpre_all, mn_all, dm_all, vec,
):
    for wc in range(2):
        base = wc * 784
        field[base : base + 168, :] = above_ref[wc].astype(F32)
        field[base + 168 : base + 560, :] = res0_ref[wc].astype(F32)
        field[base + 560 : base + 784, :] = res1_ref[wc, 0:224, :].astype(F32)
    vec[...] = jnp.zeros_like(vec)
    sg, sb, be, br = row(sg_ref), row(sb_ref), row(be_ref), row(br_ref)

    def chunk(i, carry):
        starts = []
        for rp, cp in QUADRANTS:
            for j in range(7):
                starts.append(pl.multiple_of(tile_start(0, 2 * j + cp) + (2 * i + rp) * 56, 8))
        x = jnp.concatenate([field[pl.ds(s, 8), :] for s in starts], 0)
        xhat, rstd = norm_stats(x)
        sn = (xhat * sg + sb).astype(BF16)
        here = pl.multiple_of(i * 224, 16)
        sn_all[pl.ds(here, 224), :] = sn
        hidden, slope = gelu_pair(dot(sn, we_ref[...]) + be)
        hidden = hidden.astype(BF16)
        hid_all[pl.ds(here, 224), :] = hidden
        out = (x + dot(hidden, wr_ref[...]) + br).astype(BF16).astype(F32)
        gathered = jnp.concatenate([out[56 * q : 56 * q + 56, :] for q in range(4)], 1)
        mhat, mrstd = norm_stats(gathered)
        mg = row(mg_ref)
        mn = mhat * mg + row(mb_ref)
        merged = dot(mn.astype(BF16), wm_ref[...])
        pad = pl.multiple_of(i * 64, 64)
        mn_all[pl.ds(pad, 64), :] = jnp.concatenate([mn, jnp.zeros((8, 1024), F32)], 0).astype(BF16)
        for s in range(4):
            merged_ref[s, i] = merged[:, 128 * s : 128 * s + 128].astype(BF16)
        dm32 = jnp.concatenate([cot_ref[s, i].astype(F32) for s in range(4)], 1)
        dm_all[pl.ds(pad, 64), :] = jnp.concatenate([dm32, jnp.zeros((8, 512), F32)], 0).astype(BF16)
        dmn = dot_nt(dm32.astype(BF16), wm_ref[...]).astype(BF16).astype(F32)
        vec[4:5, :] += jnp.sum(dmn * mhat, 0, keepdims=True)
        vec[5:6, :] += jnp.sum(dmn, 0, keepdims=True)
        dgathered = norm_back(dmn * mg, mhat, mrstd)
        dbo32 = jnp.concatenate([dgathered[:, 256 * q : 256 * q + 256] for q in range(4)], 0)
        dbo = dbo32.astype(BF16)
        dbo32 = dbo.astype(F32)
        dbo_all[pl.ds(here, 224), :] = dbo
        vec[3:4, 0:256] += jnp.sum(dbo32, 0, keepdims=True)
        dpre32 = dot_nt(dbo, wr_ref[...]) * slope
        vec[2:3, :] += jnp.sum(dpre32, 0, keepdims=True)
        dpre = dpre32.astype(BF16)
        dpre_all[pl.ds(here, 224), :] = dpre
        dsn = dot_nt(dpre, we_ref[...]).astype(BF16).astype(F32)
        vec[0:1, 0:256] += jnp.sum(dsn * xhat, 0, keepdims=True)
        vec[1:2, 0:256] += jnp.sum(dsn, 0, keepdims=True)
        dx = dbo32 + norm_back(dsn * sg, xhat, rstd)
        for n, s in enumerate(starts):
            field[pl.ds(s, 8), :] = dx[8 * n : 8 * n + 8, :]
        return carry

    lax.fori_loop(0, 7, chunk, 0)
    for wc in range(2):
        base = wc * 784
        dabove_ref[wc] = field[base : base + 168, :].astype(BF16)
        d0_ref[wc] = field[base + 168 : base + 560, :].astype(BF16)
        d1_ref[wc] = field[base + 560 : base + 784, :].astype(BF16)
    for s in range(8):
        dwe_ref[s] = dot_tn(sn_all[...], dpre_all[:, 128 * s : 128 * s + 128]).astype(BF16)
    dwr = dot_tn(hid_all[...], dbo_all[...])
    for s in range(2):
        dwr_ref[s] = dwr[:, 128 * s : 128 * s + 128].astype(BF16)
    dwm = dot_tn(mn_all[...], dm_all[...])
    for s in range(4):
        dwm_ref[s] = dwm[:, 128 * s : 128 * s + 128].astype(BF16)
    vec_ref[...] = vec[...]


def post(above, res0, res1, cot, *params):
    outs = [
        ((4, 7, 56, 128), BF16),
        ((2, 168, 256), BF16),
        ((2, CELLS, 256), BF16),
        ((2, 224, 256), BF16),
        ((8, 256, 128), BF16),
        ((2, 1024, 128), BF16),
        ((4, 1024, 128), BF16),
        ((8, 1024), F32),
    ]
    ins = (above, res0, res1, cot) + params
    return pl.pallas_call(
        post_kernel,
        grid=(1,),
        in_specs=[whole(a.shape) for a in ins],
        out_specs=[whole(s) for s, _ in outs],
        out_shape=[jax.ShapeDtypeStruct(s, t) for s, t in outs],
        scratch_shapes=[
            pltpu.VMEM((1568, 256), F32),
            pltpu.VMEM((1568, 256), BF16),
            pltpu.VMEM((1568, 1024), BF16),
            pltpu.VMEM((1568, 256), BF16),
            pltpu.VMEM((1568, 1024), BF16),
            pltpu.VMEM((448, 1024), BF16),
            pltpu.VMEM((448, 512), BF16),
            pltpu.VMEM((8, 1024), F32),
        ],
        compiler_params=pltpu.CompilerParams(vmem_limit_bytes=56 * MIB),
        cost_estimate=pl.CostEstimate(flops=15 * 10**9, bytes_accessed=20 * 10**6, transcendentals=3200000),
    )(*ins)


def split_frames_kernel(cot_ref, out_ref, field):
    for f in range(36):
        for i in range(7):
            start = (f * 7 + i) * 8
            field[start : start + 7, :] = cot_ref[f % 32, i].astype(F32)
    for d in range(4):
        for i in range(7):
            tiles = [
                field[pl.ds(((8 * d + 4) * 7 + i) * 8 + j, 8, stride=56), :] for j in range(7)
            ]
            out_ref[d, i] = jnp.concatenate(tiles, 0).astype(BF16)


def split_frames(cotangent):
    return pl.pallas_call(
        split_frames_kernel,
        out_shape=jax.ShapeDtypeStruct((4, 7, 56, 128), BF16),
        scratch_shapes=[pltpu.VMEM((2016, 128), F32)],
    )(cotangent)


def join_frames_kernel(parts_ref, out_ref, field):
    for d in range(4):
        for i in range(7):
            tiles = parts_ref[d, i].astype(F32)
            for j in range(7):
                field[pl.ds(((8 * d + 4) * 7 + i) * 8 + j, 8, stride=56), :] = tiles[8 * j : 8 * j + 8]
    for f in range(32):
        source = f + 32 if f < 4 else f
        for i in range(7):
            start = (source * 7 + i) * 8
            out_ref[f, i] = field[start : start + 7, :].astype(BF16)


def join_frames(parts):
    return pl.pallas_call(
        join_frames_kernel,
        out_shape=jax.ShapeDtypeStruct((32, 7, 7, 128), BF16),
        scratch_shapes=[pltpu.VMEM((2016, 128), F32)],
    )(parts)


def moved(value, axis, steps):
    sizes = [lax.axis_size(a) for a in axis]
    total = math.prod(sizes)
    pairs = []
    for source in range(total):
        if len(axis) == 1:
            pairs.append((source, (source + steps) % total))
        else:
            t, h = divmod(source, sizes[1])
            pairs.append((source, ((t + steps) % sizes[0]) * sizes[1] + (h + steps) % sizes[1]))
    return lax.ppermute(value, axis if len(axis) > 1 else axis[0], pairs)


TM = ("tm",)
ROWS = ("height",)
BOTH = ("tm", "height")


def spread_sum(slabs, factor):
    n = slabs.shape[0] // 128
    parts = lax.all_to_all(slabs.reshape(128, n, 128), BOTH, 0, 0, tiled=True)
    total = (jnp.sum(parts.astype(F32), 0) * factor).astype(BF16)
    copies = jnp.broadcast_to(total[None], (128, n, 128))
    return lax.all_to_all(copies, BOTH, 0, 0, tiled=True).reshape(128 * n, 128)


def local(
    tokens, region_ids, first_gain, first_bias, input_weight, input_bias, output_weight, output_bias,
    second_gain, second_bias, expand_weight, expand_bias, reduce_weight, reduce_bias, merge_gain, merge_bias,
    merge_weight, cotangent,
):
    merged_count = cotangent.shape[0] * cotangent.shape[1] * cotangent.shape[2] * lax.axis_size("height")
    factor = 1.0 / math.sqrt(merged_count)

    from_tm = moved(tokens[:4, 3:], TM, -1)
    from_rows = moved(tokens[4:, :3], ROWS, -1)
    from_both = moved(tokens[:4, :3], BOTH, -1)
    field = jnp.concatenate(
        [
            jnp.concatenate([tokens[4:, 3:], from_rows], 1),
            jnp.concatenate([from_tm, from_both], 1),
        ],
        0,
    )
    labels = region_ids.reshape(8, 2, 7, 2, 7).transpose(1, 3, 2, 4, 0).reshape(4, CELLS, 1)
    cot = lax.all_to_all(split_frames(cotangent), "tm", 0, 0, tiled=True)

    attn = (first_gain, first_bias, input_weight, input_bias, output_weight, output_bias)
    res1, x1, qkv1, ctx1, eq1 = attend(1, field, labels, *attn)
    above = moved(res1[:, 224:], ROWS, 1)
    res0, x0, qkv0, ctx0, eq0 = attend(0, field, labels, *attn)
    merged_parts, dabove, d0, d1, dwe, dwr, dwm, vec_post = post(
        above, res0, res1, cot, second_gain, second_bias, expand_weight, expand_bias, reduce_weight,
        reduce_bias, merge_gain, merge_bias, merge_weight,
    )
    below = moved(dabove, ROWS, -1)
    merged = join_frames(lax.all_to_all(merged_parts, "tm", 0, 0, tiled=True))

    back = (first_gain, first_bias, input_weight, output_weight)
    g0, dwi0, dwo0, vec0 = attend_back(0, d0, x0, qkv0, ctx0, eq0, labels, *back)
    g1, dwi1, dwo1, vec1 = attend_back(
        1, jnp.concatenate([d1, below], 1), x1, qkv1, ctx1, eq1, labels, *back
    )

    grad = jnp.concatenate([g0, g1], 1)
    to_tm = moved(grad[4:, :11], TM, 1)
    to_rows = moved(grad[:4, 11:], ROWS, 1)
    to_both = moved(grad[4:, 11:], BOTH, 1)
    grad_tokens = jnp.concatenate(
        [
            jnp.concatenate([to_both, to_tm], 1),
            jnp.concatenate([to_rows, grad[:4, :11]], 1),
        ],
        0,
    )

    vec_attn = vec0 + vec1
    vectors = jnp.concatenate(
        [
            vec_attn[0, :256],
            vec_attn[1, :256],
            vec_attn[2],
            vec_attn[3, :256],
            vec_post[0, :256],
            vec_post[1, :256],
            vec_post[2],
            vec_post[3, :256],
            vec_post[4],
            vec_post[5],
        ]
    ).reshape(42, 128)
    slabs = jnp.concatenate(
        [
            dwe.reshape(2048, 128),
            dwr.reshape(2048, 128),
            dwm.reshape(4096, 128),
            (dwi0 + dwi1).astype(BF16).reshape(1536, 128),
            (dwo0 + dwo1).astype(BF16).reshape(512, 128),
            jnp.pad(vectors, ((0, 1024 - 42), (0, 0))).astype(BF16),
        ],
        0,
    )
    sums = spread_sum(slabs, factor).astype(F32)

    def unslab(start, count, rows):
        part = sums[start : start + count * rows].reshape(count, rows, 128)
        return part.transpose(1, 0, 2).reshape(rows, count * 128)

    flat = sums[10240:10282].reshape(42 * 128)
    ends = [256, 512, 1280, 1536, 1792, 2048, 3072, 3328, 4352]
    vecs = jnp.split(flat, ends)
    return (
        merged,
        grad_tokens,
        vecs[0],
        vecs[1],
        unslab(8192, 6, 256),
        vecs[2],
        unslab(9728, 2, 256),
        vecs[3],
        vecs[4],
        vecs[5],
        unslab(0, 8, 256),
        vecs[6],
        unslab(2048, 2, 1024),
        vecs[7],
        vecs[8],
        vecs[9],
        unslab(4096, 4, 1024),
    )


def solution(mesh):
    in_specs = (
        (P("tm", "height", None, None), P("tm", "height", None))
        + (P(),) * 15
        + (P(None, "height", None, "tm"),)
    )
    out_specs = (P(None, "height", None, "tm"), P("tm", "height", None, None)) + (P(),) * 15
    return jax.shard_map(local, mesh=mesh, in_specs=in_specs, out_specs=out_specs, check_vma=False)
```

```python
import functools
import math

import jax
import jax.numpy as jnp
from jax import lax
from jax.experimental import pallas as pl
from jax.experimental.pallas import tpu as pltpu
from jax.sharding import PartitionSpec as P

F32 = jnp.float32
BF16 = jnp.bfloat16
NORM_EPS = 1e-05
DIM = 256
CELLS = 392
TILES = 49
FAR = 2.0**100
SCORE_SCALE = math.log2(math.e) / math.sqrt(32.0)
MIB = 1 << 20


def dot(a, b):
    return lax.dot_general(a, b, (((1,), (0,)), ((), ())), preferred_element_type=F32)


def dot_nt(a, b):
    return lax.dot_general(a, b, (((1,), (1,)), ((), ())), preferred_element_type=F32)


def dot_tn(a, b):
    return lax.dot_general(a, b, (((0,), (0,)), ((), ())), preferred_element_type=F32)


def row(ref):
    return ref[...].reshape(1, -1)


def norm_stats(x):
    average = jnp.mean(x, -1, keepdims=True)
    centred = x - average
    rstd = lax.rsqrt(jnp.mean(centred * centred, -1, keepdims=True) + NORM_EPS)
    return centred * rstd, rstd


def norm_back(dxhat, xhat, rstd):
    first = jnp.mean(dxhat, -1, keepdims=True)
    second = jnp.mean(dxhat * xhat, -1, keepdims=True)
    return (dxhat - first - xhat * second) * rstd


def lanes(rows):
    return lax.broadcasted_iota(jnp.int32, (rows, 128), 1)


def head_mask(index):
    return (lanes(1) // 32 == index).astype(BF16)


def three_parts(value, lane, start):
    high = value.astype(BF16).astype(F32)
    middle = (value - high).astype(BF16).astype(F32)
    low = value - high - middle
    return jnp.where(lane < start + 8, high, jnp.where(lane < start + 16, middle, low))


def attend_kernel(
    tok_ref, lab_ref, gain_ref, bias_ref, wi_ref, bi_ref, wo_ref, bo_ref,
    res_ref, x_ref, qkv_ref, ctx_ref, eq_ref, field,
):
    win = pl.program_id(0)

    @pl.when(win == 0)
    def spread():
        for f in range(8):
            for r in range(7):
                start = (f * 7 + r) * 16
                cells = tok_ref[f, r].astype(F32)
                for half in range(2):
                    field[half, start : start + 14, :] = cells[:, 128 * half : 128 * half + 128]

    def window():
        parts = []
        for wi in range(7):
            for wj in range(7):
                column = lax.rem(win * 7 + wj + 3, 14)
                parts.append(
                    jnp.concatenate(
                        [field[s, pl.ds(wi * 16 + column, 8, stride=112), :] for s in range(2)],
                        1,
                    )
                )
        x = jnp.concatenate(parts, 0)
        x_ref[0] = x.astype(BF16)
        xhat, _ = norm_stats(x)
        normed = (xhat * row(gain_ref) + row(bias_ref)).astype(BF16)
        packed = dot(normed, wi_ref[...]) + row(bi_ref)
        q = (packed[:, 0:256] * SCORE_SCALE).astype(BF16)
        k = packed[:, 256:512].astype(BF16)
        v = packed[:, 512:768]
        vb = v.astype(BF16)
        vs = (v * (2.0**-12)).astype(BF16)
        qkv_ref[0, :, 0:256] = q
        qkv_ref[0, :, 256:512] = k
        qkv_ref[0, :, 512:768] = vb
        label = lab_ref[0]
        lane = lanes(CELLS)
        same = lane == label
        eq32 = jnp.where(same | (lane == 27), 1.0, 0.0)
        eq = eq32.astype(BF16)
        ek = jnp.where(
            lane < 27, jnp.where(same, 0.0, -FAR), jnp.where(lane == 27, -1.0, 0.0)
        ).astype(BF16)
        ones = jnp.ones((CELLS, 128), BF16)
        sums = jnp.ones((CELLS, 128), F32)
        halves = []
        for t in range(2):
            qt = q[:, 128 * t : 128 * t + 128]
            kaug = jnp.concatenate([k[:, 128 * t : 128 * t + 128], ek], 1)
            vaug = jnp.concatenate([vs[:, 128 * t : 128 * t + 128], ones], 1)
            half = jnp.zeros((CELLS, 128), F32)
            for hh in range(4):
                h = 4 * t + hh
                qaug = jnp.concatenate([qt * head_mask(hh), eq], 1)
                p = jnp.exp2(dot_nt(qaug, kaug)).astype(BF16)
                pv = dot(p, vaug)
                total = pv[:, 128:256]
                half = jnp.where(lane // 32 == hh, pv[:, 0:128] * (4096.0 / total), half)
                sums = jnp.where((lane >= 32) & (lane < 56) & (lane % 8 == h), total, sums)
            halves.append(half)
        ctx = jnp.concatenate(halves, 1).astype(BF16)
        ctx_ref[0] = ctx
        minus = three_parts(-jnp.log2(sums), lane, 32)
        eq_ref[0] = jnp.where((lane >= 32) & (lane < 56), minus, eq32).astype(BF16)
        attended = (dot(ctx, wo_ref[...]) + row(bo_ref)).astype(BF16)
        res_ref[0] = (x + attended.astype(F32)).astype(BF16)

    window()


def on_device(kernel, outs, ins, scratch, limit, flops, steps=1, in_blocks=None, out_blocks=None):
    def specs(arrays, blocks):
        found = [pl.BlockSpec(a, lambda i, n=len(a): (0,) * n) for a in arrays]
        for at, how in (blocks or {}).items():
            found[at] = pl.BlockSpec(*how) if how else pl.BlockSpec(memory_space=pl.ANY)
        return found

    return pl.pallas_call(
        kernel,
        grid=(steps,),
        in_specs=specs([a.shape for a in ins], in_blocks),
        out_specs=specs([a for a, _ in outs], out_blocks),
        out_shape=[pltpu.HBM(s, t) for s, t in outs],
        scratch_shapes=[pltpu.SemaphoreType.DMA(s) if t is None else pltpu.VMEM(s, t) for s, t in scratch],
        compiler_params=pltpu.CompilerParams(vmem_limit_bytes=limit * MIB),
        cost_estimate=pl.CostEstimate(flops=flops, bytes_accessed=4 * 10**6, transcendentals=0),
    )(*[pltpu.with_memory_space_constraint(a, pltpu.HBM) for a in ins])


def by_window(rows, width):
    return (1, rows, width), lambda i: (i, 0, 0)


def attend(row_win, *ins):
    widths = [256, 256, 768, 256, 128]
    outs = [((2, CELLS, width), BF16) for width in widths]
    in_blocks = {
        0: ((8, 7, 14, 256), lambda i: (0, row_win, 0, 0)),
        1: ((1, CELLS, 1), lambda i: (2 * row_win + i, 0, 0)),
    }
    out_blocks = {n: by_window(CELLS, width) for n, width in enumerate(widths)}
    scratch = [((2, 896, 128), F32)]
    return on_device(attend_kernel, outs, ins, scratch, 40, 4 * 10**9, 2, in_blocks, out_blocks)


def attend_back_kernel(last, *refs):
    if last:
        (d_ref, below_ref, x_ref, qkv_ref, ctx_ref, eq_ref, lab_ref, gain_ref, bias_ref, wi_ref, wo_ref,
         dwi_ref, dwo_ref, vec_ref, post_ref, out_ref, slab_ref, field, dwi, dwo, vec) = refs
    else:
        (d_ref, x_ref, qkv_ref, ctx_ref, eq_ref, lab_ref, gain_ref, bias_ref, wi_ref, wo_ref,
         out_ref, dwi, dwo, vec, field) = refs

    win = pl.program_id(0)

    @pl.when(win == 0)
    def start():
        dwi[...] = dwi_ref[...] if last else jnp.zeros_like(dwi)
        dwo[...] = dwo_ref[...] if last else jnp.zeros_like(dwo)
        vec[...] = vec_ref[...] if last else jnp.zeros_like(vec)

    def window():
        d = jnp.concatenate([d_ref[0], below_ref[0]], 0) if last else d_ref[0]
        d32 = d.astype(F32)
        ctx = ctx_ref[0]
        dwo[...] += dot_tn(ctx, d)
        vec[3:4, 0:256] += jnp.sum(d32, 0, keepdims=True)
        dctx = dot_nt(d, wo_ref[...]).astype(BF16)
        product = dctx.astype(F32) * ctx.astype(F32)
        high = product.astype(BF16)
        low = (product - high.astype(F32)).astype(BF16)
        picks_r = lax.broadcasted_iota(jnp.int32, (256, 128), 0) // 32
        picks_c = lax.broadcasted_iota(jnp.int32, (256, 128), 1)
        picks = ((picks_c < 24) & (picks_c % 8 == picks_r)).astype(BF16)
        lane = lanes(CELLS)
        delta = three_parts(-(dot(high, picks) + dot(low, picks)), lane, 0)
        dd = jnp.where(lane < 24, delta, 0.0).astype(BF16)
        eq = eq_ref[0]
        same = lane == lab_ref[0]
        ek = jnp.where(lane < 27, jnp.where(same, 0.0, -FAR), jnp.where(lane == 27, -1.0, 0.0))
        lane1 = lanes(1)
        dqs, dks, dvs = [], [], []
        for t in range(2):
            cols = slice(128 * t, 128 * t + 128)
            qt = qkv_ref[0, :, 128 * t : 128 * t + 128]
            kt = qkv_ref[0, :, 256 + 128 * t : 256 + 128 * t + 128]
            vt = qkv_ref[0, :, 512 + 128 * t : 512 + 128 * t + 128]
            dot_t = dctx[:, cols]
            qaug = jnp.concatenate([qt, eq], 1)
            daug = jnp.concatenate([dot_t, dd], 1)
            ktt = jnp.transpose(kt.astype(F32)).astype(BF16)
            dk = jnp.zeros((CELLS, 128), F32)
            dv = jnp.zeros((CELLS, 128), F32)
            dqt = []
            for hh in range(4):
                h = 4 * t + hh
                mask = head_mask(hh)
                picked = (lane1 >= 32) & (lane1 < 56) & (lane1 % 8 == h)
                kaug = jnp.concatenate([kt * mask, jnp.where(picked, 1.0, ek).astype(BF16)], 1)
                tail = jnp.where((lane < 24) & (lane % 8 == h), 1.0, 0.0).astype(BF16)
                vaug = jnp.concatenate([vt * mask, tail], 1)
                p = jnp.exp2(dot_nt(kaug, qaug))
                ds = (p * dot_nt(vaug, daug)).astype(BF16)
                dv = dv + dot(p.astype(BF16), dot_t * mask)
                dk = dk + dot(ds, qt * mask)
                dqt.append(dot(ktt[32 * hh : 32 * hh + 32, :], ds))
            dqs.append(jnp.transpose(jnp.concatenate(dqt, 0)))
            dks.append(dk)
            dvs.append(dv)
        dpacked32 = jnp.concatenate(
            [d_q * (1.0 / math.sqrt(32.0)) for d_q in dqs]
            + [d_k * math.log(2.0) for d_k in dks]
            + dvs,
            1,
        )
        dpacked = dpacked32.astype(BF16)
        vec[2:3, :] += jnp.sum(dpacked32, 0, keepdims=True)
        x = x_ref[0].astype(F32)
        xhat, rstd = norm_stats(x)
        gain = row(gain_ref)
        normed = (xhat * gain + row(bias_ref)).astype(BF16)
        dwi[...] += dot_tn(normed, dpacked)
        dnormed = dot_nt(dpacked, wi_ref[...]).astype(BF16).astype(F32)
        vec[0:1, 0:256] += jnp.sum(dnormed * xhat, 0, keepdims=True)
        vec[1:2, 0:256] += jnp.sum(dnormed, 0, keepdims=True)
        dx = norm_back(dnormed * gain, xhat, rstd).astype(BF16).astype(F32) + d32
        for wi in range(7):
            for wj in range(7):
                column = lax.rem(win * 7 + wj + 3, 14)
                at = (wi * 7 + wj) * 8
                for s in range(2):
                    field[s, pl.ds(wi * 16 + column, 8, stride=112), :] = dx[at : at + 8, 128 * s : 128 * s + 128]

    window()

    @pl.when(win == 1)
    def finish():
        finish_back(last, refs, out_ref, field, dwi, dwo, vec)


def finish_back(last, refs, out_ref, field, dwi, dwo, vec):
    if last:
        post_ref, slab_ref = refs[14], refs[16]
    for f in range(8):
        for r in range(7):
            start = (f * 7 + r) * 16
            halves = [field[s, start : start + 14, :] for s in range(2)]
            out_ref[f, r] = jnp.concatenate(halves, 1).astype(BF16)
    if last:
        for n in range(128):
            rows = slice(16 * (n % 16), 16 * (n % 16) + 16)
            first = 128 * (n // 16)
            source = dwi[rows, first : first + 128] if n < 96 else dwo[rows, first - 768 : first - 640]
            slab_ref[n, 0:16, :] = source.astype(BF16)
        tiles = [vec[:, 128 * c : 128 * c + 128] for c in range(6)]
        tiles += [post_ref[:, 128 * c : 128 * c + 128] for c in range(8)]
        for n in range(128):
            tile = tiles[n] if n < 14 else jnp.zeros((8, 128), F32)
            slab_ref[n, 16:24, :] = tile.astype(BF16)


LATE = 24
EARLY = 64


def attend_back(row_win, given, saved, labels, params, sums):
    last = row_win == 1
    sum_shapes = [((256, 768), F32), ((256, 256), F32), ((8, 768), F32)]
    outs = [((8, 7, 14, 256), BF16)] + ([((128, LATE, 128), BF16)] if last else sum_shapes)
    ins = tuple(given) + tuple(saved) + (labels,) + tuple(params) + tuple(sums)
    scratch = [((2, 896, 128), F32)] + (sum_shapes if last else [])
    in_blocks = {n: by_window(*a.shape[1:]) for n, a in enumerate(tuple(given) + tuple(saved))}
    in_blocks[len(in_blocks)] = ((1, CELLS, 1), lambda i: (2 * row_win + i, 0, 0))
    kernel = functools.partial(attend_back_kernel, last)
    return on_device(kernel, outs, ins, scratch, 40, 6 * 10**9, 2, in_blocks)


def gelu_pair(v):
    half_square = jnp.exp2(v * v * (-0.5 * math.log2(math.e)))
    t = 1.0 / (1.0 + jnp.abs(v) * (0.3275911 * math.sqrt(0.5)))
    poly = t * (0.5 * 0.254829592 + t * (0.5 * -0.284496736 + t * (0.5 * 1.421413741 + t * (0.5 * -1.453152027 + t * (0.5 * 1.061405429)))))
    tail = poly * half_square
    phi = jnp.where(v >= 0.0, 1.0 - tail, tail)
    return v * phi, phi + v * half_square * (1.0 / math.sqrt(2.0 * math.pi))


QUADRANTS = ((0, 0), (1, 0), (0, 1), (1, 1))


def tile_start(r, c):
    s = (c - 3) % 14
    return ((s // 7) * 14 + r) * 56 + (s % 7) * 8


KEPT = ((256, 224), (1024, 224), (256, 224), (1024, 224), (1024, 64), (512, 64))


def post_chunks(first, count, field, params, merged_ref, cot_ref, kept, vec):
    sg_ref, sb_ref, we_ref, be_ref, wr_ref, br_ref, mg_ref, mb_ref, wm_ref = params
    sn_all, hid_all, dbo_all, dpre_all, mn_all, dm_all = kept
    sg, sb, be, br = row(sg_ref), row(sb_ref), row(be_ref), row(br_ref)

    def chunk(i, carry):
        starts = []
        for rp, cp in QUADRANTS:
            for j in range(7):
                starts.append(pl.multiple_of(tile_start(0, 2 * j + cp) + (2 * i + rp) * 56, 8))
        x = jnp.concatenate([field[pl.ds(s, 8), :] for s in starts], 0)
        xhat, rstd = norm_stats(x)
        sn = (xhat * sg + sb).astype(BF16)
        here = pl.multiple_of(i * 224, 16)
        sn_all[pl.ds(here, 224), :] = sn
        hidden, slope = gelu_pair(dot(sn, we_ref[...]) + be)
        hidden = hidden.astype(BF16)
        hid_all[pl.ds(here, 224), :] = hidden
        out = (x + dot(hidden, wr_ref[...]) + br).astype(BF16).astype(F32)
        gathered = jnp.concatenate([out[56 * q : 56 * q + 56, :] for q in range(4)], 1)
        mhat, mrstd = norm_stats(gathered)
        mg = row(mg_ref)
        mn = mhat * mg + row(mb_ref)
        merged = dot(mn.astype(BF16), wm_ref[...])
        pad = pl.multiple_of(i * 64, 64)
        mn_all[pl.ds(pad, 64), :] = jnp.concatenate([mn, jnp.zeros((8, 1024), F32)], 0).astype(BF16)
        for s in range(4):
            merged_ref[s, i] = merged[:, 128 * s : 128 * s + 128].astype(BF16)
        dm32 = jnp.concatenate([cot_ref[s, i].astype(F32) for s in range(4)], 1)
        dm_all[pl.ds(pad, 64), :] = jnp.concatenate([dm32, jnp.zeros((8, 512), F32)], 0).astype(BF16)
        dmn = dot_nt(dm32.astype(BF16), wm_ref[...]).astype(BF16).astype(F32)
        vec[4:5, :] += jnp.sum(dmn * mhat, 0, keepdims=True)
        vec[5:6, :] += jnp.sum(dmn, 0, keepdims=True)
        dgathered = norm_back(dmn * mg, mhat, mrstd)
        dbo32 = jnp.concatenate([dgathered[:, 256 * q : 256 * q + 256] for q in range(4)], 0)
        dbo = dbo32.astype(BF16)
        dbo32 = dbo.astype(F32)
        dbo_all[pl.ds(here, 224), :] = dbo
        vec[3:4, 0:256] += jnp.sum(dbo32, 0, keepdims=True)
        dpre32 = dot_nt(dbo, wr_ref[...]) * slope
        vec[2:3, :] += jnp.sum(dpre32, 0, keepdims=True)
        dpre = dpre32.astype(BF16)
        dpre_all[pl.ds(here, 224), :] = dpre
        dsn = dot_nt(dpre, we_ref[...]).astype(BF16).astype(F32)
        vec[0:1, 0:256] += jnp.sum(dsn * xhat, 0, keepdims=True)
        vec[1:2, 0:256] += jnp.sum(dsn, 0, keepdims=True)
        dx = dbo32 + norm_back(dsn * sg, xhat, rstd)
        for n, s in enumerate(starts):
            field[pl.ds(s, 8), :] = dx[8 * n : 8 * n + 8, :]
        return carry

    lax.fori_loop(first, first + count, chunk, 0)


def post_first_kernel(above_ref, res0_ref, cot_ref, *refs):
    params, (merged_ref, dabove_ref, d0_ref), kept = refs[:9], refs[9:12], refs[12:18]
    vec, field = refs[18:]
    for wc in range(2):
        field[wc * 784 : wc * 784 + 168, :] = above_ref[wc].astype(F32)
        field[wc * 784 + 168 : wc * 784 + 224, :] = res0_ref[wc, 0:56, :].astype(F32)
    vec[...] = jnp.zeros_like(vec)
    post_chunks(0, 2, field, params, merged_ref, cot_ref, kept, vec)
    for wc in range(2):
        dabove_ref[wc] = field[wc * 784 : wc * 784 + 168, :].astype(BF16)
        d0_ref[wc] = field[wc * 784 + 168 : wc * 784 + 224, :]


def post_second_kernel(res0_ref, res1_ref, cot_ref, *refs):
    params, (vec_in_ref, merged_in_ref, d0_in_ref), brought = refs[:9], refs[9:12], refs[12:18]
    (merged_ref, d0_ref, d1_ref, slab_ref, vec), field, kept, sems = refs[18:23], refs[23], refs[24:30], refs[30]
    copies = []
    for n, (source, target) in enumerate(zip(brought, kept, strict=True)):
        rows = source.shape[0]
        copies.append(pltpu.make_async_copy(source, target.at[0:rows], sems.at[n]))
        copies[-1].start()
    for wc in range(2):
        base = wc * 784
        field[base + 168 : base + 560, :] = res0_ref[wc].astype(F32)
        field[base + 560 : base + 784, :] = res1_ref[wc, 0:224, :].astype(F32)
    vec[...] = vec_in_ref[...]
    merged_ref[:, 0:2] = merged_in_ref[...]
    post_chunks(2, 5, field, params, merged_ref, cot_ref, kept, vec)
    for wc in range(2):
        base = wc * 784
        field[base + 168 : base + 224, :] = d0_in_ref[wc]
        d0_ref[wc] = field[base + 168 : base + 560, :].astype(BF16)
        d1_ref[wc] = field[base + 560 : base + 784, :].astype(BF16)
    for copy in copies:
        copy.wait()
    sn_all, hid_all, dbo_all, dpre_all, mn_all, dm_all = kept
    dwe = dot_tn(sn_all[...], dpre_all[...])
    for s in range(8):
        slab_ref[256 * s : 256 * s + 256, :] = dwe[:, 128 * s : 128 * s + 128].astype(BF16)
    dwr = dot_tn(hid_all[...], dbo_all[...])
    for s in range(2):
        start = 2048 + 1024 * s
        slab_ref[start : start + 1024, :] = dwr[:, 128 * s : 128 * s + 128].astype(BF16)
    dwm = dot_tn(mn_all[...], dm_all[...])
    for s in range(4):
        start = 4096 + 1024 * s
        slab_ref[start : start + 1024, :] = dwm[:, 128 * s : 128 * s + 128].astype(BF16)


def kept_shapes(chunks):
    return [((chunks * rows, width), BF16) for width, rows in KEPT]


def post_first(above, res0, cot, params):
    outs = [((4, 2, 56, 128), BF16), ((2, 168, 256), BF16), ((2, 56, 256), F32)]
    outs += kept_shapes(2) + [((8, 1024), F32)]
    in_blocks = {
        1: ((2, 64, 256), lambda i: (0, 0, 0)),
        2: ((4, 2, 56, 128), lambda i: (0, 0, 0, 0)),
    }
    scratch = [((1568, 256), F32)]
    ins = (above, res0, cot) + params
    return on_device(post_first_kernel, outs, ins, scratch, 50, 4 * 10**9, 1, in_blocks)


def post_second(res0, res1, cot, params, vec, merged, d0, brought):
    outs = [
        ((4, 7, 56, 128), BF16),
        ((2, CELLS, 256), BF16),
        ((2, 224, 256), BF16),
        ((8192, 128), BF16),
        ((8, 1024), F32),
    ]
    scratch = [((1568, 256), F32)] + kept_shapes(7) + [((6,), None)]
    ins = (res0, res1, cot) + params + (vec, merged, d0) + tuple(brought)
    in_blocks = {n: None for n in range(15, 21)}
    return on_device(post_second_kernel, outs, ins, scratch, 50, 11 * 10**9, 1, in_blocks)


def split_frames_kernel(cot_ref, out_ref, field):
    for f in range(36):
        for i in range(7):
            start = (f * 7 + i) * 8
            field[start : start + 7, :] = cot_ref[f % 32, i].astype(F32)
    for d in range(4):
        for i in range(7):
            tiles = [
                field[pl.ds(((8 * d + 4) * 7 + i) * 8 + j, 8, stride=56), :] for j in range(7)
            ]
            out_ref[d, i] = jnp.concatenate(tiles, 0).astype(BF16)


def split_frames(cotangent):
    outs = [((4, 7, 56, 128), BF16)]
    return on_device(split_frames_kernel, outs, (cotangent,), [((2016, 128), F32)], 16, 10**6)[0]


def join_frames_kernel(p0_ref, p1_ref, p2_ref, p3_ref, out_ref, field):
    me = lax.axis_index("tm")
    for back, ref in enumerate((p0_ref, p1_ref, p2_ref, p3_ref)):
        source = lax.rem(me + 4 - back, 4)
        for i in range(7):
            tiles = ref[i].astype(F32)
            for j in range(7):
                field[pl.ds(source * 448 + 224 + i * 8 + j, 8, stride=56), :] = tiles[8 * j : 8 * j + 8]
    for f in range(32):
        source = f + 32 if f < 4 else f
        for i in range(7):
            start = (source * 7 + i) * 8
            out_ref[f, i] = field[start : start + 7, :].astype(BF16)


def join_frames(*parts):
    outs = [((32, 7, 7, 128), BF16)]
    return on_device(join_frames_kernel, outs, parts, [((2016, 128), F32)], 16, 10**6)[0]


def moved(value, axis, steps):
    sizes = [lax.axis_size(a) for a in axis]
    total = math.prod(sizes)
    pairs = []
    for source in range(total):
        if len(axis) == 1:
            pairs.append((source, (source + steps) % total))
        else:
            t, h = divmod(source, sizes[1])
            pairs.append((source, ((t + steps) % sizes[0]) * sizes[1] + (h + steps) % sizes[1]))
    return lax.ppermute(value, axis if len(axis) > 1 else axis[0], pairs)


TM = ("tm",)
ROWS = ("height",)
BOTH = ("tm", "height")


def total_of(parts_ref, rows, factor):
    total = parts_ref[0, rows, :].astype(F32)
    for n in range(1, 128):
        total = total + parts_ref[n, rows, :].astype(F32)
    return (total * factor).astype(BF16)


def sum_early_kernel(factor, parts_ref, late_ref, out_ref, total):
    @pl.when(pl.program_id(0) == 0)
    def start():
        total[...] = total_of(parts_ref, slice(0, EARLY), factor)

    core = lax.rem(pl.program_id(0), 2)
    half = total[pl.ds(pl.multiple_of(core * HALF, HALF), HALF), :]
    for n in range(32):
        out_ref[n, 0:HALF, :] = half
        out_ref[n, HALF : HALF + LATE, :] = late_ref[n]


HALF = EARLY // 2


def sum_early(factor, *ins):
    outs = [((128, HALF + LATE, 128), BF16)]
    scratch = [((EARLY, 128), BF16)]
    part = lambda rows: ((32, rows, 128), lambda i: (i, 0, 0))
    kernel = functools.partial(sum_early_kernel, factor)
    return on_device(kernel, outs, ins, scratch, 24, 10**6, 4, {1: part(LATE)}, {0: part(HALF + LATE)})[0]


def sum_late_kernel(factor, parts_ref, out_ref):
    total = total_of(parts_ref, slice(HALF, HALF + LATE), factor)
    for n in range(128):
        out_ref[n] = total


def exchange(parts):
    return lax.all_to_all(parts, BOTH, 0, 0, tiled=True)


def unpack_early_kernel(own_ref, other_ref, dwe_ref, dwr_ref, dwm_ref):
    core = lax.rem(lax.axis_index("tm"), 2)
    for ref, place in ((own_ref, core), (other_ref, 1 - core)):
        shift = pl.multiple_of(place * HALF, HALF)
        for n in range(128):
            tile = ref[n, 0:HALF, :].astype(F32)
            if n < 32:
                rows, c, out = EARLY * (n % 4), n // 4, dwe_ref
            elif n < 64:
                rows, c, out = EARLY * (n % 16), n // 16 - 2, dwr_ref
            else:
                rows, c, out = EARLY * (n % 16), n // 16 - 4, dwm_ref
            out[pl.ds(rows + shift, HALF), 128 * c : 128 * c + 128] = tile


VECTORS = ((0, 0, 2), (1, 0, 2), (2, 0, 6), (3, 0, 2), (0, 6, 2), (1, 6, 2), (2, 6, 8), (3, 6, 2), (4, 6, 8), (5, 6, 8))


def unpack_late_kernel(slab_ref, dwi_ref, dwo_ref, *vec_refs):
    for n in range(128):
        tile = slab_ref[n, 0:16, :].astype(F32)
        rows = slice(16 * (n % 16), 16 * (n % 16) + 16)
        first = 128 * (n // 16)
        if n < 96:
            dwi_ref[rows, first : first + 128] = tile
        else:
            dwo_ref[rows, first - 768 : first - 640] = tile
    tiles = [slab_ref[n, 16:24, :].astype(F32) for n in range(14)]
    for (at, first, count), ref in zip(VECTORS, vec_refs, strict=True):
        rows = [tiles[first + c][at : at + 1, :] for c in range(count)]
        ref[...] = jnp.concatenate(rows, 1).reshape(128 * count)


def unpack(kernel, slabs, shapes):
    return on_device(kernel, [(s, F32) for s in shapes], slabs, [], 32, 10**6)


def rotate_frames(parts, order):
    me = lax.axis_index("tm")
    taken = [lax.dynamic_index_in_dim(parts, lax.rem(me + k, 4), 0, keepdims=False) for k in range(4)]
    return [taken[0]] + [moved(taken[k], TM, k) for k in range(1, 4)]


def local(
    tokens, region_ids, first_gain, first_bias, input_weight, input_bias, output_weight, output_bias,
    second_gain, second_bias, expand_weight, expand_bias, reduce_weight, reduce_bias, merge_gain, merge_bias,
    merge_weight, cotangent,
):
    merged_count = cotangent.shape[0] * cotangent.shape[1] * cotangent.shape[2] * lax.axis_size("height")
    factor = 1.0 / math.sqrt(merged_count)

    from_tm = moved(tokens[:4, 3:], TM, -1)
    from_rows = moved(tokens[4:, :3], ROWS, -1)
    from_both = moved(tokens[:4, :3], BOTH, -1)
    field = jnp.concatenate(
        [
            jnp.concatenate([tokens[4:, 3:], from_rows], 1),
            jnp.concatenate([from_tm, from_both], 1),
        ],
        0,
    )
    labels = region_ids.reshape(8, 2, 7, 2, 7).transpose(1, 3, 2, 4, 0).reshape(4, CELLS, 1)
    cot = lax.all_to_all(split_frames(cotangent), "tm", 0, 0, tiled=True)

    attn = (first_gain, first_bias, input_weight, input_bias, output_weight, output_bias)
    res1, x1, qkv1, ctx1, eq1 = attend(1, field, labels, *attn)
    above = moved(res1[:, 224:], ROWS, 1)
    res0, x0, qkv0, ctx0, eq0 = attend(0, field, labels, *attn)
    params = (
        second_gain, second_bias, expand_weight, expand_bias, reduce_weight, reduce_bias, merge_gain, merge_bias,
        merge_weight,
    )
    merged_first, dabove, d0_first, *kept, vec_first = post_first(above, res0, cot, params)
    below = moved(dabove, ROWS, -1)
    merged_parts, d0, d1, early, vec_post = post_second(
        res0, res1, cot, params, vec_first, merged_first, d0_first, kept
    )
    below, early = lax.optimization_barrier((below, early))
    early_parts = exchange(early.reshape(128, EARLY, 128))
    merged_pieces = rotate_frames(merged_parts, 1)

    back = (first_gain, first_bias, input_weight, output_weight)
    g0, *sums = attend_back(0, (d0,), (x0, qkv0, ctx0, eq0), labels, back, ())
    g1, late = attend_back(1, (d1, below), (x1, qkv1, ctx1, eq1), labels, back, sums + [vec_post])
    early_parts, merged_pieces = lax.optimization_barrier((early_parts, merged_pieces))
    second = exchange(sum_early(factor, early_parts, late))

    pieces = (
        moved(g0[4:], TM, 1),
        moved(g1[4:, :4], TM, 1),
        moved(g1[:4, 4:], ROWS, 1),
        moved(g1[4:, 4:], BOTH, 1),
    )

    second, pieces = lax.optimization_barrier((second, pieces))
    others = lax.ppermute(second[:, :HALF], "tm", [(0, 1), (1, 0), (2, 3), (3, 2)])
    (third,) = on_device(
        functools.partial(sum_late_kernel, factor), [((128, LATE, 128), BF16)], (second,), [], 24, 10**6
    )
    third = exchange(third)
    merged = join_frames(*merged_pieces)
    to_tm0, to_tm1, to_rows, to_both = pieces
    grad_tokens = jnp.concatenate(
        [
            jnp.concatenate([to_both, to_tm0, to_tm1], 1),
            jnp.concatenate([to_rows, g0[:4], g1[:4, :4]], 1),
        ],
        0,
    )
    dwe, dwr, dwm = unpack(unpack_early_kernel, (second, others), [(256, 1024), (1024, 256), (1024, 512)])
    third, dwe, dwr, dwm, merged, grad_tokens = lax.optimization_barrier(
        (third, dwe, dwr, dwm, merged, grad_tokens)
    )
    lengths = [(128 * count,) for _, _, count in VECTORS]
    dwi, dwo, *vecs = unpack(unpack_late_kernel, (third,), [(256, 768), (256, 256)] + lengths)
    return (
        merged, grad_tokens, vecs[0], vecs[1], dwi, vecs[2], dwo, vecs[3], vecs[4], vecs[5], dwe, vecs[6], dwr,
        vecs[7], vecs[8], vecs[9], dwm,
    )


def solution(mesh):
    in_specs = (
        (P("tm", "height", None, None), P("tm", "height", None))
        + (P(),) * 15
        + (P(None, "height", None, "tm"),)
    )
    out_specs = (P(None, "height", None, "tm"), P("tm", "height", None, None)) + (P(),) * 15
    return jax.shard_map(local, mesh=mesh, in_specs=in_specs, out_specs=out_specs, check_vma=False)
```

```python
import functools
import math

import jax
import jax.numpy as jnp
from jax import lax
from jax.experimental import pallas as pl
from jax.experimental.pallas import tpu as pltpu
from jax.sharding import PartitionSpec as P

F32 = jnp.float32
BF16 = jnp.bfloat16
NORM_EPS = 1e-05
DIM = 256
CELLS = 392
TILES = 49
FAR = 2.0**100
SCORE_SCALE = math.log2(math.e) / math.sqrt(32.0)
MIB = 1 << 20


def dot(a, b):
    return lax.dot_general(a, b, (((1,), (0,)), ((), ())), preferred_element_type=F32)


def dot_nt(a, b):
    return lax.dot_general(a, b, (((1,), (1,)), ((), ())), preferred_element_type=F32)


def dot_tn(a, b):
    return lax.dot_general(a, b, (((0,), (0,)), ((), ())), preferred_element_type=F32)


def row(ref):
    return ref[...].reshape(1, -1)


def norm_stats(x):
    average = jnp.mean(x, -1, keepdims=True)
    centred = x - average
    rstd = lax.rsqrt(jnp.mean(centred * centred, -1, keepdims=True) + NORM_EPS)
    return centred * rstd, rstd


def norm_back(dxhat, xhat, rstd):
    first = jnp.mean(dxhat, -1, keepdims=True)
    second = jnp.mean(dxhat * xhat, -1, keepdims=True)
    return (dxhat - first - xhat * second) * rstd


def lanes(rows):
    return lax.broadcasted_iota(jnp.int32, (rows, 128), 1)


def head_mask(index):
    return (lanes(1) // 32 == index).astype(BF16)


def three_parts(value, lane, start):
    high = value.astype(BF16).astype(F32)
    middle = (value - high).astype(BF16).astype(F32)
    low = value - high - middle
    return jnp.where(lane < start + 8, high, jnp.where(lane < start + 16, middle, low))


def attend_kernel(
    tok_ref, lab_ref, gain_ref, bias_ref, wi_ref, bi_ref, wo_ref, bo_ref,
    res_ref, x_ref, qkv_ref, ctx_ref, eq_ref,
):
    win = pl.program_id(0)

    def window():
        parts = []
        for wi in range(7):
            for wj in range(7):
                parts.append(tok_ref[wi, lax.rem(win * 7 + wj + 3, 14)].astype(F32))
        x = jnp.concatenate(parts, 0)
        x_ref[0] = x.astype(BF16)
        xhat, _ = norm_stats(x)
        normed = (xhat * row(gain_ref) + row(bias_ref)).astype(BF16)
        packed = dot(normed, wi_ref[...]) + row(bi_ref)
        q = (packed[:, 0:256] * SCORE_SCALE).astype(BF16)
        k = packed[:, 256:512].astype(BF16)
        v = packed[:, 512:768]
        vb = v.astype(BF16)
        vs = (v * (2.0**-12)).astype(BF16)
        qkv_ref[0, :, 0:256] = q
        qkv_ref[0, :, 256:512] = k
        qkv_ref[0, :, 512:768] = vb
        label = lab_ref[0]
        lane = lanes(CELLS)
        same = lane == label
        eq32 = jnp.where(same | (lane == 27), 1.0, 0.0)
        eq = eq32.astype(BF16)
        ek = jnp.where(
            lane < 27, jnp.where(same, 0.0, -FAR), jnp.where(lane == 27, -1.0, 0.0)
        ).astype(BF16)
        ones = jnp.ones((CELLS, 128), BF16)
        sums = jnp.ones((CELLS, 128), F32)
        halves = []
        for t in range(2):
            qt = q[:, 128 * t : 128 * t + 128]
            kaug = jnp.concatenate([k[:, 128 * t : 128 * t + 128], ek], 1)
            vaug = jnp.concatenate([vs[:, 128 * t : 128 * t + 128], ones], 1)
            half = jnp.zeros((CELLS, 128), F32)
            for hh in range(4):
                h = 4 * t + hh
                qaug = jnp.concatenate([qt * head_mask(hh), eq], 1)
                p = jnp.exp2(dot_nt(qaug, kaug)).astype(BF16)
                pv = dot(p, vaug)
                total = pv[:, 128:256]
                half = jnp.where(lane // 32 == hh, pv[:, 0:128] * (4096.0 / total), half)
                sums = jnp.where((lane >= 32) & (lane < 56) & (lane % 8 == h), total, sums)
            halves.append(half)
        ctx = jnp.concatenate(halves, 1).astype(BF16)
        ctx_ref[0] = ctx
        minus = three_parts(-jnp.log2(sums), lane, 32)
        eq_ref[0] = jnp.where((lane >= 32) & (lane < 56), minus, eq32).astype(BF16)
        attended = (dot(ctx, wo_ref[...]) + row(bo_ref)).astype(BF16)
        res_ref[0] = (x + attended.astype(F32)).astype(BF16)

    window()


def on_device(kernel, outs, ins, scratch, limit, flops, steps=1, in_blocks=None, out_blocks=None, free=()):
    def specs(arrays, blocks):
        found = [pl.BlockSpec(a, lambda i, n=len(a): (0,) * n) for a in arrays]
        for at, how in (blocks or {}).items():
            found[at] = pl.BlockSpec(*how) if how else pl.BlockSpec(memory_space=pl.ANY)
        return found

    return pl.pallas_call(
        kernel,
        grid=(steps,),
        in_specs=specs([a.shape for a in ins], in_blocks),
        out_specs=specs([a for a, _ in outs], out_blocks),
        out_shape=[pltpu.HBM(s, t) for s, t in outs],
        scratch_shapes=[pltpu.SemaphoreType.DMA(s) if t is None else pltpu.VMEM(s, t) for s, t in scratch],
        compiler_params=pltpu.CompilerParams(vmem_limit_bytes=limit * MIB),
        cost_estimate=pl.CostEstimate(flops=flops, bytes_accessed=4 * 10**6, transcendentals=0),
    )(*[a if n in free else pltpu.with_memory_space_constraint(a, pltpu.HBM) for n, a in enumerate(ins)])


def by_window(rows, width):
    return (1, rows, width), lambda i: (i, 0, 0)


def attend(row_win, *ins):
    widths = [256, 256, 768, 256, 128]
    outs = [((2, CELLS, width), BF16) for width in widths]
    in_blocks = {
        0: ((7, 14, 8, 256), lambda i: (row_win, 0, 0, 0)),
        1: ((1, CELLS, 1), lambda i: (2 * row_win + i, 0, 0)),
    }
    out_blocks = {n: by_window(CELLS, width) for n, width in enumerate(widths)}
    return on_device(attend_kernel, outs, ins, [], 40, 4 * 10**9, 2, in_blocks, out_blocks)


def attend_back_kernel(last, *refs):
    if last:
        (d_ref, x_ref, qkv_ref, ctx_ref, eq_ref, lab_ref, gain_ref, bias_ref, wi_ref, wo_ref,
         dwi_ref, dwo_ref, vec_ref, post_ref, out_ref, keep_ref, send_ref, dwi, dwo, vec) = refs
    else:
        (d_ref, below_ref, x_ref, qkv_ref, ctx_ref, eq_ref, lab_ref, gain_ref, bias_ref, wi_ref, wo_ref,
         out_ref, dwi, dwo, vec) = refs

    win = pl.program_id(0)

    @pl.when(win == 0)
    def start():
        dwi[...] = dwi_ref[...] if last else jnp.zeros_like(dwi)
        dwo[...] = dwo_ref[...] if last else jnp.zeros_like(dwo)
        vec[...] = vec_ref[...] if last else jnp.zeros_like(vec)

    def window():
        d = d_ref[0] if last else jnp.concatenate([d_ref[0], below_ref[0]], 0)
        d32 = d.astype(F32)
        ctx = ctx_ref[0]
        dwo[...] += dot_tn(ctx, d)
        vec[3:4, 0:256] += jnp.sum(d32, 0, keepdims=True)
        dctx = dot_nt(d, wo_ref[...]).astype(BF16)
        product = dctx.astype(F32) * ctx.astype(F32)
        high = product.astype(BF16)
        low = (product - high.astype(F32)).astype(BF16)
        picks_r = lax.broadcasted_iota(jnp.int32, (256, 128), 0) // 32
        picks_c = lax.broadcasted_iota(jnp.int32, (256, 128), 1)
        picks = ((picks_c < 24) & (picks_c % 8 == picks_r)).astype(BF16)
        lane = lanes(CELLS)
        delta = three_parts(-(dot(high, picks) + dot(low, picks)), lane, 0)
        dd = jnp.where(lane < 24, delta, 0.0).astype(BF16)
        eq = eq_ref[0]
        same = lane == lab_ref[0]
        ek = jnp.where(lane < 27, jnp.where(same, 0.0, -FAR), jnp.where(lane == 27, -1.0, 0.0))
        lane1 = lanes(1)
        dqs, dks, dvs = [], [], []
        for t in range(2):
            cols = slice(128 * t, 128 * t + 128)
            qt = qkv_ref[0, :, 128 * t : 128 * t + 128]
            kt = qkv_ref[0, :, 256 + 128 * t : 256 + 128 * t + 128]
            vt = qkv_ref[0, :, 512 + 128 * t : 512 + 128 * t + 128]
            dot_t = dctx[:, cols]
            qaug = jnp.concatenate([qt, eq], 1)
            daug = jnp.concatenate([dot_t, dd], 1)
            ktt = jnp.transpose(kt.astype(F32)).astype(BF16)
            dk = jnp.zeros((CELLS, 128), F32)
            dv = jnp.zeros((CELLS, 128), F32)
            dqt = []
            for hh in range(4):
                h = 4 * t + hh
                mask = head_mask(hh)
                picked = (lane1 >= 32) & (lane1 < 56) & (lane1 % 8 == h)
                kaug = jnp.concatenate([kt * mask, jnp.where(picked, 1.0, ek).astype(BF16)], 1)
                tail = jnp.where((lane < 24) & (lane % 8 == h), 1.0, 0.0).astype(BF16)
                vaug = jnp.concatenate([vt * mask, tail], 1)
                p = jnp.exp2(dot_nt(kaug, qaug))
                ds = (p * dot_nt(vaug, daug)).astype(BF16)
                dv = dv + dot(p.astype(BF16), dot_t * mask)
                dk = dk + dot(ds, qt * mask)
                dqt.append(dot(ktt[32 * hh : 32 * hh + 32, :], ds))
            dqs.append(jnp.transpose(jnp.concatenate(dqt, 0)))
            dks.append(dk)
            dvs.append(dv)
        dpacked32 = jnp.concatenate(
            [d_q * (1.0 / math.sqrt(32.0)) for d_q in dqs]
            + [d_k * math.log(2.0) for d_k in dks]
            + dvs,
            1,
        )
        dpacked = dpacked32.astype(BF16)
        vec[2:3, :] += jnp.sum(dpacked32, 0, keepdims=True)
        x = x_ref[0].astype(F32)
        xhat, rstd = norm_stats(x)
        gain = row(gain_ref)
        normed = (xhat * gain + row(bias_ref)).astype(BF16)
        dwi[...] += dot_tn(normed, dpacked)
        dnormed = dot_nt(dpacked, wi_ref[...]).astype(BF16).astype(F32)
        vec[0:1, 0:256] += jnp.sum(dnormed * xhat, 0, keepdims=True)
        vec[1:2, 0:256] += jnp.sum(dnormed, 0, keepdims=True)
        dx = norm_back(dnormed * gain, xhat, rstd).astype(BF16).astype(F32) + d32
        for wi in range(7):
            for wj in range(7):
                at = (wi * 7 + wj) * 8
                out_ref[wi, lax.rem(win * 7 + wj + 3, 14)] = dx[at : at + 8, :].astype(BF16)

    window()

    if last:
        core = lax.rem(lax.axis_index("tm"), 2)
        pl.when((win == 1) & (core == 0))(functools.partial(pack_late, keep_ref, send_ref, dwi, dwo, vec, post_ref))
        pl.when((win == 1) & (core == 1))(functools.partial(pack_late, send_ref, keep_ref, dwi, dwo, vec, post_ref))


def pack_late(even_ref, odd_ref, dwi, dwo, vec, post_ref):
    tiles = [vec[:, 128 * c : 128 * c + 128] for c in range(6)]
    tiles += [post_ref[:, 128 * c : 128 * c + 128] for c in range(8)]
    for n in range(128):
        rows = slice(16 * (n % 16), 16 * (n % 16) + 16)
        first = 128 * (n // 16)
        source = dwi[rows, first : first + 128] if n < 96 else dwo[rows, first - 768 : first - 640]
        tile = tiles[n] if n < 14 else jnp.zeros((8, 128), F32)
        ref = odd_ref if n % 2 else even_ref
        ref[n // 2] = jnp.concatenate([source, tile], 0).astype(BF16)


LATE = 24
EARLY = 64


def attend_back(row_win, given, saved, labels, params, sums):
    last = row_win == 0
    sum_shapes = [((256, 768), F32), ((256, 256), F32), ((8, 768), F32)]
    outs = [((7, 14, 8, 256), BF16)] + ([((64, LATE, 128), BF16)] * 2 if last else sum_shapes)
    ins = tuple(given) + tuple(saved) + (labels,) + tuple(params) + tuple(sums)
    scratch = sum_shapes if last else []
    in_blocks = {n: by_window(*a.shape[1:]) for n, a in enumerate(tuple(given) + tuple(saved))}
    in_blocks[len(in_blocks)] = ((1, CELLS, 1), lambda i: (2 * row_win + i, 0, 0))
    kernel = functools.partial(attend_back_kernel, last)
    return on_device(kernel, outs, ins, scratch, 40, 6 * 10**9, 2, in_blocks, free=() if last else (1,))


def gelu_pair(v):
    half_square = jnp.exp2(v * v * (-0.5 * math.log2(math.e)))
    t = 1.0 / (1.0 + jnp.abs(v) * (0.3275911 * math.sqrt(0.5)))
    poly = t * (0.5 * 0.254829592 + t * (0.5 * -0.284496736 + t * (0.5 * 1.421413741 + t * (0.5 * -1.453152027 + t * (0.5 * 1.061405429)))))
    tail = poly * half_square
    phi = jnp.where(v >= 0.0, 1.0 - tail, tail)
    return v * phi, phi + v * half_square * (1.0 / math.sqrt(2.0 * math.pi))


QUADRANTS = ((0, 0), (1, 0), (0, 1), (1, 1))


def tile_start(r, c):
    s = (c - 3) % 14
    return ((s // 7) * 14 + r) * 56 + (s % 7) * 8


KEPT = ((256, 224), (1024, 224), (256, 224), (1024, 224), (1024, 64), (512, 64))


def post_chunks(groups, field, params, merged_ref, cot_ref, kept, vec):
    sg_ref, sb_ref, we_ref, be_ref, wr_ref, br_ref, mg_ref, mb_ref, wm_ref = params
    sn_all, hid_all, dbo_all, dpre_all, mn_all, dm_all = kept
    sg, sb, be, br = row(sg_ref), row(sb_ref), row(be_ref), row(br_ref)

    def chunk(first, count):
        starts = []
        for n in range(count):
            for rp, cp in QUADRANTS:
                for j in range(7):
                    starts.append(pl.multiple_of(tile_start(0, 2 * j + cp) + (2 * (first + n) + rp) * 56, 8))
        x = jnp.concatenate([field[pl.ds(s, 8), :] for s in starts], 0)
        xhat, rstd = norm_stats(x)
        sn = (xhat * sg + sb).astype(BF16)
        here = pl.ds(pl.multiple_of(first * 224, 32), 224 * count)
        sn_all[here, :] = sn
        hidden, slope = gelu_pair(dot(sn, we_ref[...]) + be)
        hidden = hidden.astype(BF16)
        hid_all[here, :] = hidden
        out = (x + dot(hidden, wr_ref[...]) + br).astype(BF16).astype(F32)

        def patches(value, n):
            return [value[224 * n + 56 * q : 224 * n + 56 * q + 56, :] for q in range(4)]

        gathered = jnp.concatenate([jnp.concatenate(patches(out, n), 1) for n in range(count)], 0)
        mhat, mrstd = norm_stats(gathered)
        mg = row(mg_ref)
        mn = mhat * mg + row(mb_ref)
        merged = dot(mn.astype(BF16), wm_ref[...])
        dm32 = jnp.concatenate(
            [
                jnp.concatenate([cot_ref[s, first + n].astype(F32) for s in range(4)], 1)
                for n in range(count)
            ],
            0,
        )
        for n in range(count):
            rows = slice(56 * n, 56 * n + 56)
            pad = pl.ds(pl.multiple_of((first + n) * 64, 64), 64)
            mn_all[pad, :] = jnp.concatenate([mn[rows], jnp.zeros((8, 1024), F32)], 0).astype(BF16)
            dm_all[pad, :] = jnp.concatenate([dm32[rows], jnp.zeros((8, 512), F32)], 0).astype(BF16)
            for s in range(4):
                merged_ref[s, first + n] = merged[rows, 128 * s : 128 * s + 128].astype(BF16)
        dmn = dot_nt(dm32.astype(BF16), wm_ref[...]).astype(BF16).astype(F32)
        vec[4:5, :] += jnp.sum(dmn * mhat, 0, keepdims=True)
        vec[5:6, :] += jnp.sum(dmn, 0, keepdims=True)
        dgathered = norm_back(dmn * mg, mhat, mrstd)
        dbo32 = jnp.concatenate(
            [
                dgathered[56 * n : 56 * n + 56, 256 * q : 256 * q + 256]
                for n in range(count)
                for q in range(4)
            ],
            0,
        )
        dbo = dbo32.astype(BF16)
        dbo32 = dbo.astype(F32)
        dbo_all[here, :] = dbo
        vec[3:4, 0:256] += jnp.sum(dbo32, 0, keepdims=True)
        dpre32 = dot_nt(dbo, wr_ref[...]) * slope
        vec[2:3, :] += jnp.sum(dpre32, 0, keepdims=True)
        dpre = dpre32.astype(BF16)
        dpre_all[here, :] = dpre
        dsn = dot_nt(dpre, we_ref[...]).astype(BF16).astype(F32)
        vec[0:1, 0:256] += jnp.sum(dsn * xhat, 0, keepdims=True)
        vec[1:2, 0:256] += jnp.sum(dsn, 0, keepdims=True)
        dx = dbo32 + norm_back(dsn * sg, xhat, rstd)
        for n, s in enumerate(starts):
            field[pl.ds(s, 8), :] = dx[8 * n : 8 * n + 8, :]

    for first, count in groups:
        chunk(first, count)


def post_first_kernel(above_ref, res0_ref, cot_ref, *refs):
    params, (merged_ref, dabove_ref, d0_ref), kept = refs[:9], refs[9:12], refs[12:18]
    vec, field = refs[18:]
    for wc in range(2):
        field[wc * 784 : wc * 784 + 168, :] = above_ref[wc].astype(F32)
        field[wc * 784 + 168 : wc * 784 + 224, :] = res0_ref[wc, 0:56, :].astype(F32)
    vec[...] = jnp.zeros_like(vec)
    post_chunks(((0, 2),), field, params, merged_ref, cot_ref, kept, vec)
    for wc in range(2):
        dabove_ref[wc] = field[wc * 784 : wc * 784 + 168, :].astype(BF16)
        d0_ref[wc] = field[wc * 784 + 168 : wc * 784 + 224, :]


def post_second_kernel(res0_ref, res1_ref, cot_ref, *refs):
    params, (vec_in_ref, merged_in_ref, d0_in_ref), brought = refs[:9], refs[9:12], refs[12:18]
    (merged_ref, d0_ref, d1_ref, slab_ref, vec), field, kept, sems = refs[18:23], refs[23], refs[24:30], refs[30]
    copies = []
    for n, (source, target) in enumerate(zip(brought, kept, strict=True)):
        rows = source.shape[0]
        copies.append(pltpu.make_async_copy(source, target.at[0:rows], sems.at[n]))
        copies[-1].start()
    for wc in range(2):
        base = wc * 784
        field[base + 168 : base + 560, :] = res0_ref[wc].astype(F32)
        field[base + 560 : base + 784, :] = res1_ref[wc, 0:224, :].astype(F32)
    vec[...] = vec_in_ref[...]
    merged_ref[:, 0:2] = merged_in_ref[...]
    post_chunks(((2, 2), (4, 3)), field, params, merged_ref, cot_ref, kept, vec)
    for wc in range(2):
        base = wc * 784
        field[base + 168 : base + 224, :] = d0_in_ref[wc]
        d0_ref[wc] = field[base + 168 : base + 560, :].astype(BF16)
        d1_ref[wc] = field[base + 560 : base + 784, :].astype(BF16)
    for copy in copies:
        copy.wait()
    sn_all, hid_all, dbo_all, dpre_all, mn_all, dm_all = kept
    dwe = dot_tn(sn_all[...], dpre_all[...])
    for s in range(8):
        slab_ref[256 * s : 256 * s + 256, :] = dwe[:, 128 * s : 128 * s + 128].astype(BF16)
    dwr = dot_tn(hid_all[...], dbo_all[...])
    for s in range(2):
        start = 2048 + 1024 * s
        slab_ref[start : start + 1024, :] = dwr[:, 128 * s : 128 * s + 128].astype(BF16)
    dwm = dot_tn(mn_all[...], dm_all[...])
    for s in range(4):
        start = 4096 + 1024 * s
        slab_ref[start : start + 1024, :] = dwm[:, 128 * s : 128 * s + 128].astype(BF16)


def kept_shapes(chunks):
    return [((chunks * rows, width), BF16) for width, rows in KEPT]


def post_first(above, res0, cot, params):
    outs = [((4, 2, 56, 128), BF16), ((2, 168, 256), BF16), ((2, 56, 256), F32)]
    outs += kept_shapes(2) + [((8, 1024), F32)]
    in_blocks = {
        1: ((2, 64, 256), lambda i: (0, 0, 0)),
        2: ((4, 2, 56, 128), lambda i: (0, 0, 0, 0)),
    }
    scratch = [((1568, 256), F32)]
    ins = (above, res0, cot) + params
    return on_device(post_first_kernel, outs, ins, scratch, 50, 4 * 10**9, 1, in_blocks, free=(0,))


def post_second(res0, res1, cot, params, vec, merged, d0, brought):
    outs = [
        ((4, 7, 56, 128), BF16),
        ((2, CELLS, 256), BF16),
        ((2, 224, 256), BF16),
        ((8192, 128), BF16),
        ((8, 1024), F32),
    ]
    scratch = [((1568, 256), F32)] + kept_shapes(7) + [((6,), None)]
    ins = (res0, res1, cot) + params + (vec, merged, d0) + tuple(brought)
    in_blocks = {n: None for n in range(15, 21)}
    return on_device(post_second_kernel, outs, ins, scratch, 50, 11 * 10**9, 1, in_blocks)


def early_frames():
    return lax.broadcasted_iota(jnp.int32, (8, 128), 0) < 4


def split_frames_kernel(cot_ref, out_ref):
    for i in range(7):
        tiles = [cot_ref[i, j].astype(F32) for j in range(7)]
        for d in range(4):
            after = 8 * ((d + 1) % 4)
            chosen = [
                jnp.where(early_frames(), t[after : after + 8, :], t[8 * d : 8 * d + 8, :]) for t in tiles
            ]
            out_ref[d, i] = jnp.concatenate(chosen, 0).astype(BF16)


def split_frames(cotangent):
    outs = [((4, 7, 56, 128), BF16)]
    return on_device(split_frames_kernel, outs, (cotangent,), [], 16, 10**6)[0]


def join_frames_kernel(p0_ref, p1_ref, p2_ref, p3_ref, out_ref, field):
    me = lax.axis_index("tm")
    for back, ref in enumerate((p0_ref, p1_ref, p2_ref, p3_ref)):
        field[lax.rem(me + 4 - back, 4)] = ref[...].astype(F32)
    for i in range(7):
        for j in range(7):
            rows = slice(8 * j, 8 * j + 8)
            tiles = [jnp.where(early_frames(), field[(d + 3) % 4, i, rows], field[d, i, rows]) for d in range(4)]
            out_ref[i, j] = jnp.concatenate(tiles, 0).astype(BF16)


def join_frames(*parts):
    outs = [((7, 7, 32, 128), BF16)]
    return on_device(join_frames_kernel, outs, parts, [((4, 7, 56, 128), F32)], 16, 10**6)[0]


def moved(value, axis, steps):
    sizes = [lax.axis_size(a) for a in axis]
    total = math.prod(sizes)
    pairs = []
    for source in range(total):
        if len(axis) == 1:
            pairs.append((source, (source + steps) % total))
        else:
            t, h = divmod(source, sizes[1])
            pairs.append((source, ((t + steps) % sizes[0]) * sizes[1] + (h + steps) % sizes[1]))
    return lax.ppermute(value, axis if len(axis) > 1 else axis[0], pairs)


TM = ("tm",)
ROWS = ("height",)
BOTH = ("tm", "height")


def total_of(ref, rows, factor):
    total = ref[0, rows, :].astype(F32)
    for n in range(1, ref.shape[0]):
        total = total + ref[n, rows, :].astype(F32)
    return (total * factor).astype(BF16)


def sum_early_kernel(factor, parts_ref, keep_ref, other_ref, out_ref):
    total = total_of(parts_ref, slice(0, EARLY), factor)
    for n in range(64):
        out_ref[n, 0:EARLY, :] = total
        pair = keep_ref[n].astype(F32) + other_ref[n].astype(F32)
        out_ref[n, EARLY : EARLY + LATE, :] = pair.astype(BF16)


def sum_late_kernel(factor, parts_ref, out_ref):
    total = total_of(parts_ref, slice(0, LATE), factor)
    for n in range(64):
        out_ref[n] = total


def exchange(parts):
    return lax.all_to_all(parts, BOTH, 0, 0, tiled=True)


def exchange_in_core(parts):
    groups = [[t * 32 + h for t in (core, core + 2) for h in range(32)] for core in range(2)]
    return lax.all_to_all(parts, BOTH, 0, 0, tiled=True, axis_index_groups=groups)


def swap_cores(value):
    return lax.ppermute(value, "tm", [(0, 1), (1, 0), (2, 3), (3, 2)])


def by_core(kernel, own_ref, other_ref, *outs):
    core = lax.rem(lax.axis_index("tm"), 2)
    pl.when(core == 0)(functools.partial(kernel, own_ref, other_ref, *outs))
    pl.when(core == 1)(functools.partial(kernel, other_ref, own_ref, *outs))


def unpack_early(zero_ref, one_ref, dwe_ref, dwr_ref, dwm_ref):
    for n in range(128):
        ref = one_ref if n // 32 % 2 else zero_ref
        tile = ref[32 * (n // 64) + n % 32, 0:EARLY, :].astype(F32)
        if n < 32:
            rows, c, out = EARLY * (n % 4), n // 4, dwe_ref
        elif n < 64:
            rows, c, out = EARLY * (n % 16), n // 16 - 2, dwr_ref
        else:
            rows, c, out = EARLY * (n % 16), n // 16 - 4, dwm_ref
        out[rows : rows + EARLY, 128 * c : 128 * c + 128] = tile


VECTORS = ((0, 0, 2), (1, 0, 2), (2, 0, 6), (3, 0, 2), (0, 6, 2), (1, 6, 2), (2, 6, 8), (3, 6, 2), (4, 6, 8), (5, 6, 8))


def unpack_late(zero_ref, one_ref, dwi_ref, dwo_ref, *vec_refs):
    tiles = []
    for n in range(128):
        block = (one_ref if n % 2 else zero_ref)[n // 2].astype(F32)
        rows = slice(16 * (n % 16), 16 * (n % 16) + 16)
        first = 128 * (n // 16)
        if n < 96:
            dwi_ref[rows, first : first + 128] = block[0:16]
        else:
            dwo_ref[rows, first - 768 : first - 640] = block[0:16]
        tiles.append(block[16:24])
    for (at, first, count), ref in zip(VECTORS, vec_refs, strict=True):
        rows = [tiles[first + c][at : at + 1, :] for c in range(count)]
        ref[...] = jnp.concatenate(rows, 1).reshape(128 * count)


def unpack(kernel, own, other, shapes):
    outs = [(s, F32) for s in shapes]
    return on_device(functools.partial(by_core, kernel), outs, (own, other), [], 32, 10**6, free=(0, 1))


def rotate_frames(parts, order):
    me = lax.axis_index("tm")
    taken = [lax.dynamic_index_in_dim(parts, lax.rem(me + k, 4), 0, keepdims=False) for k in range(4)]
    return [taken[0]] + [moved(taken[k], TM, k) for k in range(1, 4)]


def local(
    tokens, region_ids, first_gain, first_bias, input_weight, input_bias, output_weight, output_bias,
    second_gain, second_bias, expand_weight, expand_bias, reduce_weight, reduce_bias, merge_gain, merge_bias,
    merge_weight, cotangent,
):
    merged_count = cotangent.shape[0] * cotangent.shape[1] * cotangent.shape[2] * lax.axis_size("height")
    factor = 1.0 / math.sqrt(merged_count)

    tiles = tokens.transpose(1, 2, 0, 3)
    from_tm = moved(tiles[3:, :, :4], TM, -1)
    from_rows = moved(tiles[:3, :, 4:], ROWS, -1)
    from_both = moved(tiles[:3, :, :4], BOTH, -1)
    field = jnp.concatenate(
        [
            jnp.concatenate([from_tm, tiles[3:, :, 4:]], 2),
            jnp.concatenate([from_both, from_rows], 2),
        ],
        0,
    )
    labels = jnp.concatenate([region_ids[4:], region_ids[:4]], 0).reshape(8, 2, 7, 2, 7)
    labels = labels.transpose(1, 3, 2, 4, 0).reshape(4, CELLS, 1)
    cot = lax.all_to_all(split_frames(cotangent.transpose(1, 2, 0, 3)), "tm", 0, 0, tiled=True)

    attn = (first_gain, first_bias, input_weight, input_bias, output_weight, output_bias)
    res1, x1, qkv1, ctx1, eq1 = attend(1, field, labels, *attn)
    above = moved(res1[:, 224:], ROWS, 1)
    res0, x0, qkv0, ctx0, eq0 = attend(0, field, labels, *attn)
    params = (
        second_gain, second_bias, expand_weight, expand_bias, reduce_weight, reduce_bias, merge_gain, merge_bias,
        merge_weight,
    )
    merged_first, dabove, d0_first, *kept, vec_first = post_first(above, res0, cot, params)
    below = moved(dabove, ROWS, -1)
    merged_parts, d0, d1, early, vec_post = post_second(
        res0, res1, cot, params, vec_first, merged_first, d0_first, kept
    )
    below, early = lax.optimization_barrier((below, early))
    early_parts = exchange(early.reshape(128, EARLY, 128))
    merged_pieces = rotate_frames(merged_parts, 1)

    back = (first_gain, first_bias, input_weight, output_weight)
    g1, *sums = attend_back(1, (d1, below), (x1, qkv1, ctx1, eq1), labels, back, ())
    pieces = (moved(g1[:4, :, :4], TM, 1), moved(g1[4:, :, 4:], ROWS, 1), moved(g1[4:, :, :4], BOTH, 1))
    g0, late_keep, late_send = attend_back(0, (d0,), (x0, qkv0, ctx0, eq0), labels, back, sums + [vec_post])
    late_other = swap_cores(late_send)
    kernel = functools.partial(sum_early_kernel, factor)
    outs = [((64, EARLY + LATE, 128), BF16)]
    ins = (early_parts, late_keep, late_other)
    (second,) = on_device(kernel, outs, ins, [], 24, 10**6, free=(0, 1, 2))
    second = exchange_in_core(second)
    to_tm0 = moved(g0[:, :, :4], TM, 1)

    to_tm1, to_rows, to_both = pieces
    second, to_tm0, to_tm1, merged_pieces = lax.optimization_barrier((second, to_tm0, to_tm1, merged_pieces))
    others = swap_cores(second)
    kernel = functools.partial(sum_late_kernel, factor)
    (third,) = on_device(
        kernel, [((64, LATE, 128), BF16)], (second[:, EARLY:],), [], 16, 10**6, free=(0,)
    )
    third = exchange_in_core(third)
    merged = join_frames(*merged_pieces)
    dwe, dwr, dwm = unpack(unpack_early, second, others, [(256, 1024), (1024, 256), (1024, 512)])
    third, to_rows, to_both, dwe, dwr, dwm, merged = lax.optimization_barrier(
        (third, to_rows, to_both, dwe, dwr, dwm, merged)
    )
    grad_tiles = jnp.concatenate(
        [
            jnp.concatenate([to_both, to_rows], 2),
            jnp.concatenate([to_tm0, g0[:, :, 4:]], 2),
            jnp.concatenate([to_tm1, g1[:4, :, 4:]], 2),
        ],
        0,
    )
    third_other = swap_cores(third)
    merged, grad_tokens = merged.transpose(2, 0, 1, 3), grad_tiles.transpose(2, 0, 1, 3)
    lengths = [(128 * count,) for _, _, count in VECTORS]
    dwi, dwo, *vecs = unpack(unpack_late, third, third_other, [(256, 768), (256, 256)] + lengths)
    return (
        merged, grad_tokens, vecs[0], vecs[1], dwi, vecs[2], dwo, vecs[3], vecs[4], vecs[5], dwe, vecs[6], dwr,
        vecs[7], vecs[8], vecs[9], dwm,
    )


def solution(mesh):
    in_specs = (
        (P("tm", "height", None, None), P("tm", "height", None))
        + (P(),) * 15
        + (P(None, "height", None, "tm"),)
    )
    out_specs = (P(None, "height", None, "tm"), P("tm", "height", None, None)) + (P(),) * 15
    return jax.shard_map(local, mesh=mesh, in_specs=in_specs, out_specs=out_specs, check_vma=False)
```

```python
import functools
import math

import jax
import jax.numpy as jnp
from jax import lax
from jax.experimental import pallas as pl
from jax.experimental.pallas import tpu as pltpu
from jax.sharding import PartitionSpec as P

F32 = jnp.float32
BF16 = jnp.bfloat16
NORM_EPS = 1e-05
CELLS = 392
FAR = 2.0**100
SCORE_SCALE = math.log2(math.e) / math.sqrt(32.0)
MIB = 1 << 20


def dot(a, b):
    return lax.dot_general(a, b, (((1,), (0,)), ((), ())), preferred_element_type=F32)


def dot_nt(a, b):
    return lax.dot_general(a, b, (((1,), (1,)), ((), ())), preferred_element_type=F32)


def dot_tn(a, b):
    return lax.dot_general(a, b, (((0,), (0,)), ((), ())), preferred_element_type=F32)


def row(ref):
    return ref[...].reshape(1, -1)


def norm_stats(x):
    average = jnp.mean(x, -1, keepdims=True)
    centred = x - average
    rstd = lax.rsqrt(jnp.mean(centred * centred, -1, keepdims=True) + NORM_EPS)
    return centred * rstd, rstd


def norm_back(dxhat, xhat, rstd):
    first = jnp.mean(dxhat, -1, keepdims=True)
    second = jnp.mean(dxhat * xhat, -1, keepdims=True)
    return (dxhat - first - xhat * second) * rstd


def lanes(rows):
    return lax.broadcasted_iota(jnp.int32, (rows, 128), 1)


def head_mask(index):
    return (lanes(1) // 32 == index).astype(BF16)


def three_parts(value, lane, start):
    high = value.astype(BF16).astype(F32)
    middle = (value - high).astype(BF16).astype(F32)
    low = value - high - middle
    return jnp.where(lane < start + 8, high, jnp.where(lane < start + 16, middle, low))


def attend_kernel(
    tok_ref, lab_ref, gain_ref, bias_ref, wi_ref, bi_ref, wo_ref, bo_ref,
    res_ref, tail_ref, x_ref, qkv_ref, ctx_ref, eq_ref,
):
    win = pl.program_id(0)

    def window():
        parts = []
        for wi in range(7):
            for wj in range(7):
                parts.append(tok_ref[wi, lax.rem(win * 7 + wj + 3, 14)].astype(F32))
        x = jnp.concatenate(parts, 0)
        x_ref[0] = x.astype(BF16)
        xhat, _ = norm_stats(x)
        normed = (xhat * row(gain_ref) + row(bias_ref)).astype(BF16)
        packed = dot(normed, wi_ref[...]) + row(bi_ref)
        q = (packed[:, 0:256] * SCORE_SCALE).astype(BF16)
        k = packed[:, 256:512].astype(BF16)
        v = packed[:, 512:768]
        vb = v.astype(BF16)
        vs = (v * (2.0**-12)).astype(BF16)
        qkv_ref[0, :, 0:256] = q
        qkv_ref[0, :, 256:512] = k
        qkv_ref[0, :, 512:768] = vb
        label = lab_ref[0]
        lane = lanes(CELLS)
        same = lane == label
        eq32 = jnp.where(same | (lane == 27), 1.0, 0.0)
        eq = eq32.astype(BF16)
        ek = jnp.where(
            lane < 27, jnp.where(same, 0.0, -FAR), jnp.where(lane == 27, -1.0, 0.0)
        ).astype(BF16)
        ones = jnp.ones((CELLS, 128), BF16)
        sums = jnp.ones((CELLS, 128), F32)
        halves = []
        for t in range(2):
            qt = q[:, 128 * t : 128 * t + 128]
            kaug = jnp.concatenate([k[:, 128 * t : 128 * t + 128], ek], 1)
            vaug = jnp.concatenate([vs[:, 128 * t : 128 * t + 128], ones], 1)
            half = jnp.zeros((CELLS, 128), F32)
            for hh in range(4):
                h = 4 * t + hh
                qaug = jnp.concatenate([qt * head_mask(hh), eq], 1)
                p = jnp.exp2(dot_nt(qaug, kaug)).astype(BF16)
                pv = dot(p, vaug)
                total = pv[:, 128:256]
                half = jnp.where(lane // 32 == hh, pv[:, 0:128] * (4096.0 / total), half)
                sums = jnp.where((lane >= 32) & (lane < 56) & (lane % 8 == h), total, sums)
            halves.append(half)
        ctx = jnp.concatenate(halves, 1).astype(BF16)
        ctx_ref[0] = ctx
        minus = three_parts(-jnp.log2(sums), lane, 32)
        eq_ref[0] = jnp.where((lane >= 32) & (lane < 56), minus, eq32).astype(BF16)
        attended = (dot(ctx, wo_ref[...]) + row(bo_ref)).astype(BF16)
        res = x + attended.astype(F32)
        res_ref[0] = res.astype(BF16)
        tail_ref[0] = res[224:].astype(BF16)

    window()


def on_device(kernel, outs, ins, scratch, limit, flops, steps=1, in_blocks=None, out_blocks=None, free=()):
    def specs(arrays, blocks):
        found = [pl.BlockSpec(a, lambda i, n=len(a): (0,) * n) for a in arrays]
        for at, how in (blocks or {}).items():
            found[at] = pl.BlockSpec(*how) if how else pl.BlockSpec(memory_space=pl.ANY)
        return found

    return pl.pallas_call(
        kernel,
        grid=(steps,),
        in_specs=specs([a.shape for a in ins], in_blocks),
        out_specs=specs([a for a, _ in outs], out_blocks),
        out_shape=[pltpu.HBM(s, t) for s, t in outs],
        scratch_shapes=[pltpu.SemaphoreType.DMA(s) if t is None else pltpu.VMEM(s, t) for s, t in scratch],
        compiler_params=pltpu.CompilerParams(vmem_limit_bytes=limit * MIB),
        cost_estimate=pl.CostEstimate(flops=flops, bytes_accessed=4 * 10**6, transcendentals=0),
    )(*[a if n in free else pltpu.with_memory_space_constraint(a, pltpu.HBM) for n, a in enumerate(ins)])


def by_window(rows, width):
    return (1, rows, width), lambda i: (i, 0, 0)


def attend(row_win, *ins):
    sizes = [(CELLS, 256), (168, 256), (CELLS, 256), (CELLS, 768), (CELLS, 256), (CELLS, 128)]
    outs = [((2,) + size, BF16) for size in sizes]
    in_blocks = {
        0: ((7, 14, 8, 256), lambda i: (row_win, 0, 0, 0)),
        1: ((1, CELLS, 1), lambda i: (2 * row_win + i, 0, 0)),
    }
    out_blocks = {n: by_window(*size) for n, size in enumerate(sizes)}
    return on_device(attend_kernel, outs, ins, [], 40, 4 * 10**9, 2, in_blocks, out_blocks)


def attend_back_kernel(last, *refs):
    if last:
        (d_ref, x_ref, qkv_ref, ctx_ref, eq_ref, lab_ref, gain_ref, bias_ref, wi_ref, wo_ref,
         dwi_ref, dwo_ref, vec_ref, post_ref, out_ref, keep_ref, send_ref, dwi, dwo, vec) = refs
    else:
        (d_ref, below_ref, x_ref, qkv_ref, ctx_ref, eq_ref, lab_ref, gain_ref, bias_ref, wi_ref, wo_ref,
         out_ref, dwi, dwo, vec) = refs

    win = pl.program_id(0)

    @pl.when(win == 0)
    def start():
        dwi[...] = dwi_ref[...] if last else jnp.zeros_like(dwi)
        dwo[...] = dwo_ref[...] if last else jnp.zeros_like(dwo)
        vec[...] = vec_ref[...] if last else jnp.zeros_like(vec)

    def window():
        d = d_ref[0] if last else jnp.concatenate([d_ref[0], below_ref[0]], 0)
        d32 = d.astype(F32)
        ctx = ctx_ref[0]
        dwo[...] += dot_tn(ctx, d)
        vec[3:4, 0:256] += jnp.sum(d32, 0, keepdims=True)
        dctx = dot_nt(d, wo_ref[...]).astype(BF16)
        product = dctx.astype(F32) * ctx.astype(F32)
        high = product.astype(BF16)
        low = (product - high.astype(F32)).astype(BF16)
        picks_r = lax.broadcasted_iota(jnp.int32, (256, 128), 0) // 32
        picks_c = lax.broadcasted_iota(jnp.int32, (256, 128), 1)
        picks = ((picks_c < 24) & (picks_c % 8 == picks_r)).astype(BF16)
        lane = lanes(CELLS)
        delta = three_parts(-(dot(high, picks) + dot(low, picks)), lane, 0)
        dd = jnp.where(lane < 24, delta, 0.0).astype(BF16)
        eq = eq_ref[0]
        same = lane == lab_ref[0]
        ek = jnp.where(lane < 27, jnp.where(same, 0.0, -FAR), jnp.where(lane == 27, -1.0, 0.0))
        lane1 = lanes(1)
        dqs, dks, dvs = [], [], []
        for t in range(2):
            cols = slice(128 * t, 128 * t + 128)
            qt = qkv_ref[0, :, 128 * t : 128 * t + 128]
            kt = qkv_ref[0, :, 256 + 128 * t : 256 + 128 * t + 128]
            vt = qkv_ref[0, :, 512 + 128 * t : 512 + 128 * t + 128]
            dot_t = dctx[:, cols]
            qaug = jnp.concatenate([qt, eq], 1)
            daug = jnp.concatenate([dot_t, dd], 1)
            ktt = jnp.transpose(kt.astype(F32)).astype(BF16)
            dk = jnp.zeros((CELLS, 128), F32)
            dv = jnp.zeros((CELLS, 128), F32)
            dqt = []
            for hh in range(4):
                h = 4 * t + hh
                mask = head_mask(hh)
                picked = (lane1 >= 32) & (lane1 < 56) & (lane1 % 8 == h)
                kaug = jnp.concatenate([kt * mask, jnp.where(picked, 1.0, ek).astype(BF16)], 1)
                tail = jnp.where((lane < 24) & (lane % 8 == h), 1.0, 0.0).astype(BF16)
                vaug = jnp.concatenate([vt * mask, tail], 1)
                p = jnp.exp2(dot_nt(kaug, qaug))
                ds = (p * dot_nt(vaug, daug)).astype(BF16)
                dv = dv + dot(p.astype(BF16), dot_t * mask)
                dk = dk + dot(ds, qt * mask)
                dqt.append(dot(ktt[32 * hh : 32 * hh + 32, :], ds))
            dqs.append(jnp.transpose(jnp.concatenate(dqt, 0)))
            dks.append(dk)
            dvs.append(dv)
        dpacked32 = jnp.concatenate(
            [d_q * (1.0 / math.sqrt(32.0)) for d_q in dqs]
            + [d_k * math.log(2.0) for d_k in dks]
            + dvs,
            1,
        )
        dpacked = dpacked32.astype(BF16)
        vec[2:3, :] += jnp.sum(dpacked32, 0, keepdims=True)
        x = x_ref[0].astype(F32)
        xhat, rstd = norm_stats(x)
        gain = row(gain_ref)
        normed = (xhat * gain + row(bias_ref)).astype(BF16)
        dwi[...] += dot_tn(normed, dpacked)
        dnormed = dot_nt(dpacked, wi_ref[...]).astype(BF16).astype(F32)
        vec[0:1, 0:256] += jnp.sum(dnormed * xhat, 0, keepdims=True)
        vec[1:2, 0:256] += jnp.sum(dnormed, 0, keepdims=True)
        dx = norm_back(dnormed * gain, xhat, rstd).astype(BF16).astype(F32) + d32
        for wi in range(7):
            for wj in range(7):
                at = (wi * 7 + wj) * 8
                out_ref[wi, lax.rem(win * 7 + wj + 3, 14)] = dx[at : at + 8, :].astype(BF16)

    window()

    if last:
        core = lax.rem(lax.axis_index("tm"), 2)
        pl.when((win == 1) & (core == 0))(functools.partial(pack_late, keep_ref, send_ref, dwi, dwo, vec, post_ref))
        pl.when((win == 1) & (core == 1))(functools.partial(pack_late, send_ref, keep_ref, dwi, dwo, vec, post_ref))


def pack_late(even_ref, odd_ref, dwi, dwo, vec, post_ref):
    tiles = [vec[:, 128 * c : 128 * c + 128] for c in range(6)]
    tiles += [post_ref[:, 128 * c : 128 * c + 128] for c in range(8)]
    for n in range(128):
        rows = slice(16 * (n % 16), 16 * (n % 16) + 16)
        first = 128 * (n // 16)
        source = dwi[rows, first : first + 128] if n < 96 else dwo[rows, first - 768 : first - 640]
        tile = tiles[n] if n < 14 else jnp.zeros((8, 128), F32)
        ref = odd_ref if n % 2 else even_ref
        ref[n // 2] = jnp.concatenate([source, tile], 0).astype(BF16)


LATE = 24
EARLY = 64


def attend_back(row_win, given, saved, labels, params, sums):
    last = row_win == 0
    sum_shapes = [((256, 768), F32), ((256, 256), F32), ((8, 768), F32)]
    outs = [((7, 14, 8, 256), BF16)] + ([((64, LATE, 128), BF16)] * 2 if last else sum_shapes)
    ins = tuple(given) + tuple(saved) + (labels,) + tuple(params) + tuple(sums)
    scratch = sum_shapes if last else []
    in_blocks = {n: by_window(*a.shape[1:]) for n, a in enumerate(tuple(given) + tuple(saved))}
    in_blocks[len(in_blocks)] = ((1, CELLS, 1), lambda i: (2 * row_win + i, 0, 0))
    kernel = functools.partial(attend_back_kernel, last)
    return on_device(kernel, outs, ins, scratch, 40, 6 * 10**9, 2, in_blocks, free=() if last else (1,))


def gelu_pair(v):
    half_square = jnp.exp2(v * v * (-0.5 * math.log2(math.e)))
    t = 1.0 / (1.0 + jnp.abs(v) * (0.3275911 * math.sqrt(0.5)))
    poly = t * (0.5 * 0.254829592 + t * (0.5 * -0.284496736 + t * (0.5 * 1.421413741 + t * (0.5 * -1.453152027 + t * (0.5 * 1.061405429)))))
    tail = poly * half_square
    phi = jnp.where(v >= 0.0, 1.0 - tail, tail)
    return v * phi, phi + v * half_square * (1.0 / math.sqrt(2.0 * math.pi))


QUADRANTS = ((0, 0), (1, 0), (0, 1), (1, 1))


def tile_start(r, c):
    s = (c - 3) % 14
    return ((s // 7) * 14 + r) * 56 + (s % 7) * 8


KEPT = ((256, 224), (1024, 224), (256, 224), (1024, 224), (1024, 64), (512, 64))


def post_chunks(groups, field, params, merged_ref, cot_ref, kept, vec):
    sg_ref, sb_ref, we_ref, be_ref, wr_ref, br_ref, mg_ref, mb_ref, wm_ref = params
    sn_all, hid_all, dbo_all, dpre_all, mn_all, dm_all = kept
    sg, sb, be, br = row(sg_ref), row(sb_ref), row(be_ref), row(br_ref)

    def chunk(first, count):
        starts = []
        for n in range(count):
            for rp, cp in QUADRANTS:
                for j in range(7):
                    starts.append(pl.multiple_of(tile_start(0, 2 * j + cp) + (2 * (first + n) + rp) * 56, 8))
        x = jnp.concatenate([field[pl.ds(s, 8), :] for s in starts], 0)
        xhat, rstd = norm_stats(x)
        sn = (xhat * sg + sb).astype(BF16)
        here = pl.ds(pl.multiple_of(first * 224, 32), 224 * count)
        sn_all[here, :] = sn
        hidden, slope = gelu_pair(dot(sn, we_ref[...]) + be)
        hidden = hidden.astype(BF16)
        hid_all[here, :] = hidden
        out = (x + dot(hidden, wr_ref[...]) + br).astype(BF16).astype(F32)

        def patches(value, n):
            return [value[224 * n + 56 * q : 224 * n + 56 * q + 56, :] for q in range(4)]

        gathered = jnp.concatenate([jnp.concatenate(patches(out, n), 1) for n in range(count)], 0)
        mhat, mrstd = norm_stats(gathered)
        mg = row(mg_ref)
        mn = mhat * mg + row(mb_ref)
        merged = dot(mn.astype(BF16), wm_ref[...])
        dm32 = jnp.concatenate(
            [
                jnp.concatenate([cot_ref[s, first + n].astype(F32) for s in range(4)], 1)
                for n in range(count)
            ],
            0,
        )
        for n in range(count):
            rows = slice(56 * n, 56 * n + 56)
            pad = pl.ds(pl.multiple_of((first + n) * 64, 64), 64)
            mn_all[pad, :] = jnp.concatenate([mn[rows], jnp.zeros((8, 1024), F32)], 0).astype(BF16)
            dm_all[pad, :] = jnp.concatenate([dm32[rows], jnp.zeros((8, 512), F32)], 0).astype(BF16)
            for s in range(4):
                merged_ref[s, first + n] = merged[rows, 128 * s : 128 * s + 128].astype(BF16)
        dmn = dot_nt(dm32.astype(BF16), wm_ref[...]).astype(BF16).astype(F32)
        vec[4:5, :] += jnp.sum(dmn * mhat, 0, keepdims=True)
        vec[5:6, :] += jnp.sum(dmn, 0, keepdims=True)
        dgathered = norm_back(dmn * mg, mhat, mrstd)
        dbo32 = jnp.concatenate(
            [
                dgathered[56 * n : 56 * n + 56, 256 * q : 256 * q + 256]
                for n in range(count)
                for q in range(4)
            ],
            0,
        )
        dbo = dbo32.astype(BF16)
        dbo32 = dbo.astype(F32)
        dbo_all[here, :] = dbo
        vec[3:4, 0:256] += jnp.sum(dbo32, 0, keepdims=True)
        dpre32 = dot_nt(dbo, wr_ref[...]) * slope
        vec[2:3, :] += jnp.sum(dpre32, 0, keepdims=True)
        dpre = dpre32.astype(BF16)
        dpre_all[here, :] = dpre
        dsn = dot_nt(dpre, we_ref[...]).astype(BF16).astype(F32)
        vec[0:1, 0:256] += jnp.sum(dsn * xhat, 0, keepdims=True)
        vec[1:2, 0:256] += jnp.sum(dsn, 0, keepdims=True)
        dx = dbo32 + norm_back(dsn * sg, xhat, rstd)
        for n, s in enumerate(starts):
            field[pl.ds(s, 8), :] = dx[8 * n : 8 * n + 8, :]

    for first, count in groups:
        chunk(first, count)


def post_first_kernel(above_ref, res0_ref, cot_ref, *refs):
    params, (merged_ref, dabove_ref, d0_ref), kept = refs[:9], refs[9:12], refs[12:18]
    vec, field = refs[18:]
    for wc in range(2):
        field[wc * 784 : wc * 784 + 168, :] = above_ref[wc].astype(F32)
        field[wc * 784 + 168 : wc * 784 + 224, :] = res0_ref[wc, 0:56, :].astype(F32)
    vec[...] = jnp.zeros_like(vec)
    post_chunks(((0, 2),), field, params, merged_ref, cot_ref, kept, vec)
    for wc in range(2):
        dabove_ref[wc] = field[wc * 784 : wc * 784 + 168, :].astype(BF16)
        d0_ref[wc] = field[wc * 784 + 168 : wc * 784 + 224, :]


def post_second_kernel(res0_ref, res1_ref, cot_ref, *refs):
    params, (vec_in_ref, merged_in_ref, d0_in_ref), brought = refs[:9], refs[9:12], refs[12:18]
    (merged_ref, d0_ref, d1_ref, slab_ref, vec), field, kept, sems = refs[18:23], refs[23], refs[24:30], refs[30]
    copies = []
    for n, (source, target) in enumerate(zip(brought, kept, strict=True)):
        rows = source.shape[0]
        copies.append(pltpu.make_async_copy(source, target.at[0:rows], sems.at[n]))
        copies[-1].start()
    for wc in range(2):
        base = wc * 784
        field[base + 168 : base + 560, :] = res0_ref[wc].astype(F32)
        field[base + 560 : base + 784, :] = res1_ref[wc, 0:224, :].astype(F32)
    vec[...] = vec_in_ref[...]
    merged_ref[:, 0:2] = merged_in_ref[...]
    post_chunks(((2, 2), (4, 3)), field, params, merged_ref, cot_ref, kept, vec)
    for wc in range(2):
        base = wc * 784
        field[base + 168 : base + 224, :] = d0_in_ref[wc]
        d0_ref[wc] = field[base + 168 : base + 560, :].astype(BF16)
        d1_ref[wc] = field[base + 560 : base + 784, :].astype(BF16)
    for copy in copies:
        copy.wait()
    sn_all, hid_all, dbo_all, dpre_all, mn_all, dm_all = kept
    dwe = dot_tn(sn_all[...], dpre_all[...])
    for s in range(8):
        slab_ref[256 * s : 256 * s + 256, :] = dwe[:, 128 * s : 128 * s + 128].astype(BF16)
    dwr = dot_tn(hid_all[...], dbo_all[...])
    for s in range(2):
        start = 2048 + 1024 * s
        slab_ref[start : start + 1024, :] = dwr[:, 128 * s : 128 * s + 128].astype(BF16)
    dwm = dot_tn(mn_all[...], dm_all[...])
    for s in range(4):
        start = 4096 + 1024 * s
        slab_ref[start : start + 1024, :] = dwm[:, 128 * s : 128 * s + 128].astype(BF16)


def kept_shapes(chunks):
    return [((chunks * rows, width), BF16) for width, rows in KEPT]


def post_first(above, res0, cot, params):
    outs = [((4, 2, 56, 128), BF16), ((2, 168, 256), BF16), ((2, 56, 256), F32)]
    outs += kept_shapes(2) + [((8, 1024), F32)]
    in_blocks = {
        1: ((2, 64, 256), lambda i: (0, 0, 0)),
        2: ((4, 2, 56, 128), lambda i: (0, 0, 0, 0)),
    }
    scratch = [((1568, 256), F32)]
    ins = (above, res0, cot) + params
    return on_device(post_first_kernel, outs, ins, scratch, 50, 4 * 10**9, 1, in_blocks, free=(0,))


def post_second(res0, res1, cot, params, vec, merged, d0, brought):
    outs = [
        ((4, 7, 56, 128), BF16),
        ((2, CELLS, 256), BF16),
        ((2, 224, 256), BF16),
        ((8192, 128), BF16),
        ((8, 1024), F32),
    ]
    scratch = [((1568, 256), F32)] + kept_shapes(7) + [((6,), None)]
    ins = (res0, res1, cot) + params + (vec, merged, d0) + tuple(brought)
    in_blocks = {n: None for n in range(15, 21)}
    return on_device(post_second_kernel, outs, ins, scratch, 50, 11 * 10**9, 1, in_blocks)


def early_frames():
    return lax.broadcasted_iota(jnp.int32, (8, 128), 0) < 4


def split_frames_kernel(cot_ref, out_ref):
    for i in range(7):
        tiles = [cot_ref[i, j].astype(F32) for j in range(7)]
        for d in range(4):
            after = 8 * ((d + 1) % 4)
            chosen = [
                jnp.where(early_frames(), t[after : after + 8, :], t[8 * d : 8 * d + 8, :]) for t in tiles
            ]
            out_ref[d, i] = jnp.concatenate(chosen, 0).astype(BF16)


def split_frames(cotangent):
    outs = [((4, 7, 56, 128), BF16)]
    return on_device(split_frames_kernel, outs, (cotangent,), [], 16, 10**6)[0]


def join_frames_kernel(p0_ref, p1_ref, p2_ref, p3_ref, out_ref, field):
    me = lax.axis_index("tm")
    for back, ref in enumerate((p0_ref, p1_ref, p2_ref, p3_ref)):
        field[lax.rem(me + 4 - back, 4)] = ref[...].astype(F32)
    for i in range(7):
        for j in range(7):
            rows = slice(8 * j, 8 * j + 8)
            tiles = [jnp.where(early_frames(), field[(d + 3) % 4, i, rows], field[d, i, rows]) for d in range(4)]
            out_ref[i, j] = jnp.concatenate(tiles, 0).astype(BF16)


def join_frames(*parts):
    outs = [((7, 7, 32, 128), BF16)]
    return on_device(join_frames_kernel, outs, parts, [((4, 7, 56, 128), F32)], 16, 10**6)[0]


def moved(value, axis, steps):
    sizes = [lax.axis_size(a) for a in axis]
    total = math.prod(sizes)
    pairs = []
    for source in range(total):
        if len(axis) == 1:
            pairs.append((source, (source + steps) % total))
        else:
            t, h = divmod(source, sizes[1])
            pairs.append((source, ((t + steps) % sizes[0]) * sizes[1] + (h + steps) % sizes[1]))
    return lax.ppermute(value, axis if len(axis) > 1 else axis[0], pairs)


TM = ("tm",)
ROWS = ("height",)
BOTH = ("tm", "height")


def total_of(ref, rows, factor):
    total = ref[0, rows, :].astype(F32)
    for n in range(1, ref.shape[0]):
        total = total + ref[n, rows, :].astype(F32)
    return (total * factor).astype(BF16)


def sum_early_kernel(factor, parts_ref, keep_ref, other_ref, out_ref):
    total = total_of(parts_ref, slice(0, EARLY), factor)
    for n in range(64):
        out_ref[n, 0:EARLY, :] = total
        pair = keep_ref[n].astype(F32) + other_ref[n].astype(F32)
        out_ref[n, EARLY : EARLY + LATE, :] = pair.astype(BF16)


def sum_late_kernel(factor, parts_ref, out_ref):
    total = total_of(parts_ref, slice(0, LATE), factor)
    for n in range(64):
        out_ref[n] = total


def exchange(parts):
    return lax.all_to_all(parts, BOTH, 0, 0, tiled=True)


def exchange_in_core(parts):
    groups = [[t * 32 + h for t in (core, core + 2) for h in range(32)] for core in range(2)]
    return lax.all_to_all(parts, BOTH, 0, 0, tiled=True, axis_index_groups=groups)


def swap_cores(value):
    return lax.ppermute(value, "tm", [(0, 1), (1, 0), (2, 3), (3, 2)])


def by_core(kernel, own_ref, other_ref, *outs):
    core = lax.rem(lax.axis_index("tm"), 2)
    pl.when(core == 0)(functools.partial(kernel, own_ref, other_ref, *outs))
    pl.when(core == 1)(functools.partial(kernel, other_ref, own_ref, *outs))


def unpack_early(zero_ref, one_ref, dwe_ref, dwr_ref, dwm_ref):
    for n in range(128):
        ref = one_ref if n // 32 % 2 else zero_ref
        tile = ref[32 * (n // 64) + n % 32, 0:EARLY, :].astype(F32)
        if n < 32:
            rows, c, out = EARLY * (n % 4), n // 4, dwe_ref
        elif n < 64:
            rows, c, out = EARLY * (n % 16), n // 16 - 2, dwr_ref
        else:
            rows, c, out = EARLY * (n % 16), n // 16 - 4, dwm_ref
        out[rows : rows + EARLY, 128 * c : 128 * c + 128] = tile


VECTORS = ((0, 0, 2), (1, 0, 2), (2, 0, 6), (3, 0, 2), (0, 6, 2), (1, 6, 2), (2, 6, 8), (3, 6, 2), (4, 6, 8), (5, 6, 8))


def unpack_late(zero_ref, one_ref, dwi_ref, dwo_ref, *vec_refs):
    tiles = []
    for n in range(128):
        block = (one_ref if n % 2 else zero_ref)[n // 2].astype(F32)
        rows = slice(16 * (n % 16), 16 * (n % 16) + 16)
        first = 128 * (n // 16)
        if n < 96:
            dwi_ref[rows, first : first + 128] = block[0:16]
        else:
            dwo_ref[rows, first - 768 : first - 640] = block[0:16]
        tiles.append(block[16:24])
    for (at, first, count), ref in zip(VECTORS, vec_refs, strict=True):
        rows = [tiles[first + c][at : at + 1, :] for c in range(count)]
        ref[...] = jnp.concatenate(rows, 1).reshape(128 * count)


def unpack(kernel, own, other, shapes):
    outs = [(s, F32) for s in shapes]
    return on_device(functools.partial(by_core, kernel), outs, (own, other), [], 32, 10**6, free=(0, 1))


def rotate_frames(parts, order):
    me = lax.axis_index("tm")
    taken = [lax.dynamic_index_in_dim(parts, lax.rem(me + k, 4), 0, keepdims=False) for k in range(4)]
    return [taken[0]] + [moved(taken[k], TM, k) for k in range(1, 4)]


def local(
    tokens, region_ids, first_gain, first_bias, input_weight, input_bias, output_weight, output_bias,
    second_gain, second_bias, expand_weight, expand_bias, reduce_weight, reduce_bias, merge_gain, merge_bias,
    merge_weight, cotangent,
):
    merged_count = cotangent.shape[0] * cotangent.shape[1] * cotangent.shape[2] * lax.axis_size("height")
    factor = 1.0 / math.sqrt(merged_count)

    tiles = tokens.transpose(1, 2, 0, 3)
    from_tm = moved(tiles[3:, :, :4], TM, -1)
    from_rows = moved(tiles[:3, :, 4:], ROWS, -1)
    from_both = moved(tiles[:3, :, :4], BOTH, -1)
    field = jnp.concatenate(
        [
            jnp.concatenate([from_tm, tiles[3:, :, 4:]], 2),
            jnp.concatenate([from_both, from_rows], 2),
        ],
        0,
    )
    labels = jnp.concatenate([region_ids[4:], region_ids[:4]], 0).reshape(8, 2, 7, 2, 7)
    labels = labels.transpose(1, 3, 2, 4, 0).reshape(4, CELLS, 1)
    cot = lax.all_to_all(split_frames(cotangent.transpose(1, 2, 0, 3)), "tm", 0, 0, tiled=True)

    attn = (first_gain, first_bias, input_weight, input_bias, output_weight, output_bias)
    res1, tail, x1, qkv1, ctx1, eq1 = attend(1, field, labels, *attn)
    above = moved(tail, ROWS, 1)
    res0, _, x0, qkv0, ctx0, eq0 = attend(0, field, labels, *attn)
    params = (
        second_gain, second_bias, expand_weight, expand_bias, reduce_weight, reduce_bias, merge_gain, merge_bias,
        merge_weight,
    )
    merged_first, dabove, d0_first, *kept, vec_first = post_first(above, res0, cot, params)
    below = moved(dabove, ROWS, -1)
    merged_parts, d0, d1, early, vec_post = post_second(
        res0, res1, cot, params, vec_first, merged_first, d0_first, kept
    )
    below, early = lax.optimization_barrier((below, early))
    early_parts = exchange(early.reshape(128, EARLY, 128))
    merged_pieces = rotate_frames(merged_parts, 1)

    back = (first_gain, first_bias, input_weight, output_weight)
    g1, *sums = attend_back(1, (d1, below), (x1, qkv1, ctx1, eq1), labels, back, ())
    pieces = (moved(g1[:4, :, :4], TM, 1), moved(g1[4:, :, 4:], ROWS, 1), moved(g1[4:, :, :4], BOTH, 1))
    g0, late_keep, late_send = attend_back(0, (d0,), (x0, qkv0, ctx0, eq0), labels, back, sums + [vec_post])
    late_other = swap_cores(late_send)
    kernel = functools.partial(sum_early_kernel, factor)
    outs = [((64, EARLY + LATE, 128), BF16)]
    ins = (early_parts, late_keep, late_other)
    (second,) = on_device(kernel, outs, ins, [], 24, 10**6, free=(0, 2))
    second = exchange_in_core(second)
    to_tm0 = moved(g0[:, :, :4], TM, 1)

    to_tm1, to_rows, to_both = pieces
    second, to_tm0, to_tm1, merged_pieces = lax.optimization_barrier((second, to_tm0, to_tm1, merged_pieces))
    others = swap_cores(second)
    kernel = functools.partial(sum_late_kernel, factor)
    (third,) = on_device(
        kernel, [((64, LATE, 128), BF16)], (second[:, EARLY:],), [], 16, 10**6, free=(0,)
    )
    third = exchange_in_core(third)
    merged = join_frames(*merged_pieces)
    dwe, dwr, dwm = unpack(unpack_early, second, others, [(256, 1024), (1024, 256), (1024, 512)])
    third, to_rows, to_both, dwe, dwr, dwm, merged = lax.optimization_barrier(
        (third, to_rows, to_both, dwe, dwr, dwm, merged)
    )
    grad_tiles = jnp.concatenate(
        [
            jnp.concatenate([to_both, to_rows], 2),
            jnp.concatenate([to_tm0, g0[:, :, 4:]], 2),
            jnp.concatenate([to_tm1, g1[:4, :, 4:]], 2),
        ],
        0,
    )
    third_other = swap_cores(third)
    merged, grad_tokens = merged.transpose(2, 0, 1, 3), grad_tiles.transpose(2, 0, 1, 3)
    lengths = [(128 * count,) for _, _, count in VECTORS]
    dwi, dwo, *vecs = unpack(unpack_late, third, third_other, [(256, 768), (256, 256)] + lengths)
    return (
        merged, grad_tokens, vecs[0], vecs[1], dwi, vecs[2], dwo, vecs[3], vecs[4], vecs[5], dwe, vecs[6], dwr,
        vecs[7], vecs[8], vecs[9], dwm,
    )


def solution(mesh):
    in_specs = (
        (P("tm", "height", None, None), P("tm", "height", None))
        + (P(),) * 15
        + (P(None, "height", None, "tm"),)
    )
    out_specs = (P(None, "height", None, "tm"), P("tm", "height", None, None)) + (P(),) * 15
    return jax.shard_map(local, mesh=mesh, in_specs=in_specs, out_specs=out_specs, check_vma=False)
```
